256 devices in a mesh: dp: 16 (over z, core), fsdp: 16 (over y, x).
Axes of the slice: x: 4, y: 4, z: 8, core: 2. Of those that a mesh axis runs over, the one named last changes fastest.
Arguments:
- grads: bfloat16 [16, 128, 2560, 128], P('dp', None, 'fsdp'), may hold values from -1400 to 1400
- owner: int32 [128, 1], replicated, may hold values from 0 to 15; in each aligned block of 8 rows (0 to 7, 8 to 15, ...) at most 2 rows name the same one
- momentum: float32 [16, 16, 2, 2560, 128], P('dp', 'fsdp'), may hold values from -24 to 24
Outputs:
- update: float32 [128, 2560, 128], P('dp', 'fsdp')
- new_momentum: float32 [16, 16, 2, 2560, 128], P('dp', 'fsdp')
The draws below stay inside these ranges and needn't reach their ends.
Inputs may be any that keep to these rules, and one draw needn't show every extreme that they name: Among the 8 blocks of one index of dp at most 2 have the same owner; in some index of dp one owner has exactly 2.
All inputs are finite; a program needn't handle non-finite values.
Results may differ from the reference program's by a relative error of at most 0.0003.
Values may be sent and summed in bfloat16 or wider, within the bound.
A program may use at most 64 MiB of HBM per device.

```python
import math
import jax
import jax.numpy as jnp
import numpy as np
from jax import lax

R = 128
D = 2560
MPG = 8
ITERS = 3
M = 128
CAP = 2
N_DP = 16
N_FSDP = 16


def draw_grads(key, part):
    key = jax.random.fold_in(key, 11)
    base_key, row_key, col_key = jax.random.split(key, 3)
    shape = (N_DP, M, D, R)
    rising = 3.0 ** (jnp.arange(D, dtype=jnp.float32) / D)
    row_scale = jnp.exp(jax.random.uniform(row_key, (1, M, D, 1), jnp.float32, 0.0, math.log(10.0))) * rising[None, None, :, None]
    col_scale = jnp.exp(jax.random.uniform(col_key, (1, M, 1, R), jnp.float32, 0.0, math.log(10.0)))
    noise = jnp.clip(jax.random.normal(base_key, shape, jnp.float32), -4.0, 4.0)
    return (noise * row_scale * col_scale).astype(jnp.bfloat16)


def levels(key, extent, shards, smallest, high):
    def one(axis_at, parts):
        steps = jax.random.uniform(jax.random.fold_in(jax.random.fold_in(key, 6), axis_at), (parts,), jnp.float32, smallest / len(shards), high / len(shards))
        return jnp.repeat(jnp.exp(steps), extent[axis_at] // parts).reshape((-1,) + (1,) * (len(extent) - axis_at - 1))

    factor_of = one(*shards[0])
    for cut in shards[1:]:
        factor_of = factor_of * one(*cut)
    return factor_of


def routed_block(rng, own, number, rows, amount, top, limit, slope):
    order = jax.random.permutation(rng, amount)
    heavy_load, common = shares(amount, rows * top, limit, slope, True), shares(amount, rows * top, limit, slope, False)
    places = jnp.arange(amount)

    def named(lengths, offset_by):
        used = int((lengths > 0).sum())
        fixed = max(1, used // 4)
        passed = fixed + (places - fixed + offset_by * (used - fixed)) % max(1, amount - fixed)
        return jnp.zeros((amount,), jnp.int32).at[order[jnp.where(places < fixed, places, passed)]].set(jnp.asarray(lengths, jnp.int32))

    lengths = jnp.where(number % 4 == 0, named(heavy_load, number // 4), named(common, number - number // 4 - 1))
    mixed = jax.random.permutation(jax.random.fold_in(own, 3), amount)
    giver, taker = mixed[0:amount // 2 * 2:2], mixed[1:amount // 2 * 2:2]
    margin = jnp.minimum(lengths[giver] - 1, limit - lengths[taker]) // 2
    margin = jnp.where((giver == order[0]) | (taker == order[0]) | (lengths[taker] == 0), 0, jnp.maximum(margin, 0))
    passed = jax.random.randint(jax.random.fold_in(own, 4), (amount // 2,), 0, 1 << 20) % (margin + 1)
    lengths = lengths.at[giver].add(-passed).at[taker].add(passed)
    members = jnp.searchsorted(jnp.cumsum(lengths), jnp.arange(rows * top), side="right").astype(jnp.int32)
    table = members.reshape(top, rows).T
    table = table[jax.random.permutation(jax.random.fold_in(own, 1), rows)]
    offset_by = jax.random.randint(jax.random.fold_in(own, 2), (rows, 1), 0, top)
    return jnp.take_along_axis(table, (jnp.arange(top)[None, :] + offset_by) % top, axis=1)


def shares(amount, total, reach, skew, full):
    weights = [(1 << 20) // math.isqrt(rank ** skew) + 1 for rank in range(1, amount + 1)]
    largest = reach if full else min(reach, max(-(-total // amount), total * weights[0] // sum(weights)))
    least = 1 if total - largest >= amount - 1 else 0
    given, surplus = [largest] + [least] * (amount - 1), total - largest - least * (amount - 1)
    while surplus > 0:
        free = [i for i in range(1, amount) if given[i] < largest] or [i for i in range(1, amount) if given[i] < reach]
        pool, budget = sum([weights[i] for i in free]), surplus
        for i in free:
            more = min(reach - given[i], max(1, budget * weights[i] // pool), surplus)
            given[i] = given[i] + more
            surplus = surplus - more
    return np.array(given)


def gaussian(own_key, extent, width, bound, cuts=(), kind=jnp.bfloat16):
    drawn = jax.random.normal(own_key, extent, jnp.float32) * width
    if len(cuts) > 0:
        drawn = levels(own_key, extent, cuts, -0.22, 0.18) * drawn
    return jnp.clip(drawn, min=-bound, max=bound).astype(kind)


def setup_inputs(seed: int = 0) -> dict:
    streams_of = jax.random.split(jax.random.key(seed), 4)
    grads = draw_grads(jax.random.fold_in(streams_of[3], 71), 0)
    owner_keys = jax.random.split(jax.random.fold_in(streams_of[1], 1), M // MPG)
    owner_turns = jax.random.permutation(jax.random.fold_in(streams_of[1], 3), M // MPG)
    owner = jax.vmap(lambda own, number: routed_block(jax.random.fold_in(streams_of[1], 2), own, number, MPG, N_FSDP, 1, CAP, 2))(owner_keys, owner_turns).reshape((M, 1))
    momentum = gaussian(streams_of[2], (N_DP, N_FSDP, CAP, D, R), 4.0, 24.0, ((0, 16), (1, 16)), jnp.float32)
    return dict(grads=grads, owner=owner, momentum=momentum)


COEF_A = 3.4445
COEF_B = -4.775
COEF_C = 2.0315
MOMENTUM_RATE = 0.95

def orthogonalize(velocity):
    frob_norm = jnp.sqrt(lax.optimization_barrier(jnp.sum(velocity * velocity, axis=(1, 2), keepdims=True)))
    iterate = velocity / (frob_norm + 1e-07)
    for sweep in range(ITERS):
        gram_now = jnp.einsum('mdr,mds->mrs', iterate, iterate, precision=lax.Precision.HIGHEST)
        poly_term = COEF_B * gram_now + COEF_C * jnp.einsum('mrs,mst->mrt', gram_now, gram_now, precision=lax.Precision.HIGHEST)
        iterate = COEF_A * iterate + jnp.einsum('mdr,mrs->mds', iterate, poly_term, precision=lax.Precision.HIGHEST)
    return iterate

def reference(grads, owner, momentum):
    gradient = lax.optimization_barrier(jnp.sum(grads, axis=0, dtype=jnp.float32)) / N_DP
    owner_grid = owner[:, 0].reshape(N_DP, MPG)
    columns = jnp.arange(MPG, dtype=jnp.int32)
    earlier = (owner_grid[:, :, None] == owner_grid[:, None, :]) & (columns[None, None, :] < columns[None, :, None])
    position = lax.optimization_barrier(jnp.sum(earlier.astype(jnp.int32), axis=2)).astype(jnp.int32)
    groups = jnp.broadcast_to(jnp.arange(N_DP, dtype=jnp.int32)[:, None], (N_DP, MPG))
    previous = momentum[groups, owner_grid, position].reshape(M, D, R)
    renewed = MOMENTUM_RATE * previous + gradient
    new_state = (MOMENTUM_RATE * momentum).at[groups, owner_grid, position].set(renewed.reshape(N_DP, MPG, D, R))
    velocity = gradient + MOMENTUM_RATE * renewed
    update = 0.2 * math.sqrt(D) * orthogonalize(velocity)
    return (update, new_state)
```

```python
import math

import jax
import jax.numpy as jnp
from jax import lax
from jax.experimental import pallas as pl
from jax.experimental.pallas import tpu as pltpu
from jax.sharding import PartitionSpec as P

MESH = pl.DeviceIdType.MESH
F32 = jnp.float32

NZ = 8
NY = 4
NX = 4
NF = NY * NX
BLOCKS = 8
SLOTS = 2
D = 2560
R = 128
PIECE = D // NF
CHUNK = 32
HALF = CHUNK // 2
NCH = PIECE // CHUNK
EARLY = PIECE - CHUNK
ITERS = 3

COEF_A = 3.4445
COEF_B = -4.775
COEF_C = 2.0315
RATE = 0.95

OFFSETS = ((2, 2), (0, 2), (2, 0), (1, 2), (2, 1), (3, 2), (2, 3), (1, 1), (3, 3), (1, 3), (3, 1), (0, 1), (1, 0), (0, 3), (3, 0))
SIB_ORDER = (4, 3, 5, 2, 6, 1, 7, 0)
RIGHT, LEFT = 0, 1


def dot(a, b):
    return lax.dot_general(a, b, (((1,), (0,)), ((), ())), precision=lax.Precision.HIGHEST, preferred_element_type=F32)


def dot_t(a, b):
    return lax.dot_general(a, b, (((0,), (0,)), ((), ())), precision=lax.Precision.HIGHEST, preferred_element_type=F32)


def polynomial(gram):
    rows = lax.broadcasted_iota(jnp.int32, (R, R), 0)
    cols = lax.broadcasted_iota(jnp.int32, (R, R), 1)
    eye = jnp.where(rows == cols, 1.0, 0.0).astype(F32)
    total = jnp.sum(jnp.sum(gram * eye, axis=1, keepdims=True), axis=0, keepdims=True)
    inv = 1.0 / (jnp.sqrt(total) + 1e-07)
    gram = (gram * inv) * inv
    product = None
    for sweep in range(ITERS):
        poly = COEF_A * eye + COEF_B * gram + COEF_C * dot(gram, gram)
        product = poly if product is None else dot(product, poly)
        if sweep < ITERS - 1:
            gram = dot(poly, dot(gram, poly))
    return (0.2 * math.sqrt(D)) * inv * product


def kernel(
    grads, owner, mom, update, grad_out,
    own, sib, s0, rz, mrecv, gbuf, vbuf, sendg, gsend, grecv, rrecv, qbuf, idx_tab, val_tab,
    own_sem, sib_ssem, sib_rsem, z_ssem, z_rsem, m_ssem, m_rsem, m_lsem, g_ssem, g_rsem, g_lsem,
    p_ssem, p_rsem, r_ssem, r_rsem, q_ssem, q_rsem,
):
    group = lax.axis_index("dp")
    f = lax.axis_index("fsdp")
    z, c = group // 2, group % 2
    y, x = f // NX, f % NX

    def z_of(step):
        return (z + step) % NZ

    def plane(dy, dx):
        return ((y + dy) % NY) * NX + (x + dx) % NX

    sibling = (z * 2 + 1 - c, f)
    z_dev = ((z_of(1) * 2 + c, f), (z_of(NZ - 1) * 2 + c, f))

    own_copy = [pltpu.make_async_copy(grads.at[z_of(j), c], own.at[z_of(j)], own_sem.at[j]) for j in range(NZ)]
    for j in SIB_ORDER:
        own_copy[j].start()
    mom_local = pltpu.make_async_copy(mom.at[:, pl.ds(f * PIECE, PIECE)], mrecv.at[f], m_lsem)
    mom_local.start()

    barrier = pltpu.get_barrier_semaphore()
    for peer in (sibling,) + z_dev + tuple((group, plane(dy, dx)) for dy, dx in OFFSETS):
        pl.semaphore_signal(barrier, inc=1, device_id=peer, device_id_type=MESH)

    owners = [owner[group * BLOCKS + m] for m in range(BLOCKS)]
    places = []
    for m in range(BLOCKS):
        place = jnp.int32(0)
        for earlier in range(m):
            place = place + jnp.where(owners[earlier] == owners[m], 1, 0).astype(jnp.int32)
        places.append(jnp.minimum(place, SLOTS - 1))
    keys = [owners[m] * SLOTS + places[m] for m in range(BLOCKS)]

    def table(slot, carry):
        index, valid = jnp.int32(0), jnp.float32(0)
        for m in range(BLOCKS):
            hit = keys[m] == slot
            index = jnp.where(hit, m, index)
            valid = jnp.where(hit, 1.0, valid)
        idx_tab[slot] = index
        val_tab[slot] = valid
        return carry

    lax.fori_loop(0, NF * SLOTS, table, 0)

    pl.semaphore_wait(barrier, 3 + len(OFFSETS))

    sib_copy = [
        pltpu.make_async_remote_copy(
            src_ref=grads.at[z_of(j), 1 - c], dst_ref=sib.at[z_of(j)], send_sem=sib_ssem.at[j],
            recv_sem=sib_rsem.at[j], device_id=sibling, device_id_type=MESH)
        for j in range(NZ)
    ]
    for j in SIB_ORDER:
        sib_copy[j].start()

    def send_momentum(chunk):
        row = chunk * CHUNK
        for dy, dx in OFFSETS:
            to = plane(dy, dx)
            pltpu.make_async_remote_copy(
                src_ref=mom.at[:, pl.ds(pl.multiple_of(to * PIECE + row, CHUNK), CHUNK)],
                dst_ref=mrecv.at[f, :, pl.ds(pl.multiple_of(row, CHUNK), CHUNK)],
                send_sem=m_ssem, recv_sem=m_rsem, device_id=(group, to), device_id_type=MESH).start()

    def pair_sum(at, first, count):
        rows = pl.ds(pl.multiple_of(first, 16), count)
        return own[at, :, rows, :].astype(F32) + sib[at, :, rows, :].astype(F32)

    def first_copy(d, p):
        return pltpu.make_async_remote_copy(
            src_ref=s0.at[d, p], dst_ref=rz.at[d, 0, p, :, pl.ds(HALF * d, HALF)], send_sem=z_ssem.at[d, 0, p],
            recv_sem=z_rsem.at[d, 0, p], device_id=z_dev[d], device_id_type=MESH)

    def z_copy(d, t, p):
        if t == 0:
            return first_copy(d, p)
        return pltpu.make_async_remote_copy(
            src_ref=rz.at[d, t - 1, p], dst_ref=rz.at[d, t, p], send_sem=z_ssem.at[d, t, p],
            recv_sem=z_rsem.at[d, t, p], device_id=z_dev[d], device_id_type=MESH)

    def arrive(j):
        own_copy[j].wait()
        sib_copy[j].wait_recv()

    send_momentum(jnp.int32(0))
    arrive(4)

    def start_chain(p, carry):
        for d in (RIGHT, LEFT):
            s0[d, p] = pair_sum(z_of(4), p * CHUNK + HALF * d, HALF)
            z_copy(d, 0, p).start()
        return carry

    lax.fori_loop(0, NCH, start_chain, 0)

    def hop(t, p):
        for d in (RIGHT, LEFT):
            step = 4 - t if d == RIGHT else NZ - 4 + t

            @pl.when(p == 0)
            def _():
                arrive(step)

            at = z_of(step)
            z_copy(d, t - 1, p).wait_recv()
            if t == 1:
                other = 1 - d
                rz[d, 0, p, :, HALF * d:HALF * d + HALF, :] += pair_sum(at, p * CHUNK + HALF * d, HALF)
                rz[d, 0, p, :, HALF * other:HALF * other + HALF, :] = pair_sum(at, p * CHUNK + HALF * other, HALF)
            else:
                rz[d, t - 1, p] += pair_sum(at, p * CHUNK, CHUNK)
            z_copy(d, t, p).start()

    def finish(p):
        z_copy(RIGHT, 3, p).wait_recv()
        z_copy(LEFT, 3, p).wait_recv()
        rows = pl.ds(pl.multiple_of(p * CHUNK, CHUNK), CHUNK)
        gbuf[:, rows, :] = (pair_sum(z, p * CHUNK, CHUNK) + rz[RIGHT, 3, p] + rz[LEFT, 3, p]) * (1.0 / 16.0)

    def send_gradient(p):
        rows = pl.ds(pl.multiple_of(p * CHUNK, CHUNK), CHUNK)

        def fill(to, carry):
            for s in range(SLOTS):
                sendg[to, s, rows, :] = gbuf[idx_tab[to * SLOTS + s], rows, :] * val_tab[to * SLOTS + s]
            return carry

        lax.fori_loop(0, NF, fill, 0)
        target = pl.ds(pl.multiple_of(f * PIECE + p * CHUNK, CHUNK), CHUNK)
        for dy, dx in OFFSETS:
            to = plane(dy, dx)
            pltpu.make_async_remote_copy(
                src_ref=sendg.at[to, :, rows], dst_ref=grad_out.at[:, target],
                send_sem=g_ssem, recv_sem=g_rsem, device_id=(group, to), device_id_type=MESH).start()

    def slot(s, carry):
        for t in (1, 2, 3):
            p = s - t

            @pl.when((p >= 0) & (p < NCH))
            def _():
                hop(t, p)

        @pl.when(s < NCH)
        def _():
            send_momentum(s)

        @pl.when(s == 4)
        def _():
            arrive(0)

        @pl.when(s >= 4)
        def _():
            finish(s - 4)
            send_gradient(s - 4)

        return carry

    lax.fori_loop(1, NCH + 3, slot, 0)

    pltpu.make_async_copy(mrecv.at[pl.ds(0, NF - 1)], mrecv.at[pl.ds(0, NF - 1)], m_rsem).wait()
    mom_local.wait()

    def velocity(first, count):
        for m in range(BLOCKS):
            vbuf[m, first:first + count, :] = (1.0 + RATE) * gbuf[m, first:first + count, :] + (RATE * RATE) * mrecv[
                owners[m], places[m], first:first + count, :]

    def handler(b):
        return 2 * b + c

    def gram_copy(b):
        return pltpu.make_async_remote_copy(
            src_ref=gsend.at[b], dst_ref=grecv.at[f], send_sem=p_ssem.at[b], recv_sem=p_rsem,
            device_id=(group, handler(b)), device_id_type=MESH)

    def rows_copy(b):
        return pltpu.make_async_remote_copy(
            src_ref=vbuf.at[b, pl.ds(EARLY, CHUNK)], dst_ref=rrecv.at[f], send_sem=r_ssem.at[b], recv_sem=r_rsem,
            device_id=(group, handler(b)), device_id_type=MESH)

    velocity(0, EARLY)
    for b in range(BLOCKS):
        part = vbuf[b, 0:EARLY, :]
        gsend[b] = dot_t(part, part)

        @pl.when(handler(b) != f)
        def _():
            gram_copy(b).start()

    finish(NCH - 1)
    velocity(EARLY, CHUNK)
    for b in range(BLOCKS):
        @pl.when(handler(b) != f)
        def _():
            rows_copy(b).start()

    send_gradient(NCH - 1)
    grad_local = pltpu.make_async_copy(sendg.at[f], grad_out.at[:, pl.ds(f * PIECE, PIECE)], g_lsem)
    grad_local.start()

    mine = f // 2
    handles = f % 2 == c

    def q_copy(to):
        return pltpu.make_async_remote_copy(
            src_ref=qbuf.at[mine], dst_ref=qbuf.at[mine], send_sem=q_ssem, recv_sem=q_rsem.at[mine],
            device_id=(group, to), device_id_type=MESH)

    @pl.when(handles)
    def _():
        grecv[f] = gsend[mine]
        rrecv[f] = vbuf[mine, EARLY:PIECE, :]
        pltpu.make_async_copy(grecv.at[pl.ds(0, NF - 1)], grecv.at[pl.ds(0, NF - 1)], p_rsem).wait()
        gram = grecv[0]
        for i in range(1, NF):
            gram = gram + grecv[i]
        pltpu.make_async_copy(rrecv.at[pl.ds(0, NF - 1)], rrecv.at[pl.ds(0, NF - 1)], r_rsem).wait()
        late = rrecv[...].reshape(NF * CHUNK, R)
        gram = gram + dot_t(late, late)
        qbuf[mine] = polynomial(gram)
        for dy, dx in OFFSETS:
            q_copy(plane(dy, dx)).start()

    for b in range(BLOCKS):
        @pl.when(handler(b) != f)
        def _():
            pltpu.make_async_copy(qbuf.at[b], qbuf.at[b], q_rsem.at[b]).wait()

        update[b] = dot(vbuf[b], qbuf[b])

    @pl.when(handles)
    def _():
        pltpu.make_async_copy(grecv.at[pl.ds(0, NF - 1)], grecv.at[pl.ds(0, NF - 1)], q_ssem).wait()

    for b in range(BLOCKS):
        @pl.when(handler(b) != f)
        def _():
            gram_copy(b).wait_send()
            rows_copy(b).wait_send()

    for j in range(NZ):
        sib_copy[j].wait_send()

    def drain(p, carry):
        for d in (RIGHT, LEFT):
            for t in range(4):
                z_copy(d, t, p).wait_send()
        return carry

    lax.fori_loop(0, NCH, drain, 0)
    whole = sendg.at[pl.ds(0, NF - 1)]
    pltpu.make_async_copy(whole, whole, m_ssem).wait()
    pltpu.make_async_copy(whole, whole, g_ssem).wait()
    grad_local.wait()
    pltpu.make_async_copy(whole, whole, g_rsem).wait()


def local(grads, owner, momentum):
    raw = grads[0].reshape(NZ, 2, BLOCKS, PIECE, R)
    previous = momentum[0, 0]
    dma = pltpu.SemaphoreType.DMA
    update, gathered = pl.pallas_call(
        kernel,
        out_shape=(
            jax.ShapeDtypeStruct((BLOCKS, PIECE, R), F32),
            jax.ShapeDtypeStruct((SLOTS, D, R), F32),
        ),
        in_specs=[
            pl.BlockSpec(memory_space=pl.ANY),
            pl.BlockSpec(memory_space=pltpu.SMEM),
            pl.BlockSpec(memory_space=pl.ANY),
        ],
        out_specs=(pl.BlockSpec(memory_space=pltpu.VMEM), pl.BlockSpec(memory_space=pl.ANY)),
        scratch_shapes=[
            pltpu.VMEM((NZ, BLOCKS, PIECE, R), jnp.bfloat16),
            pltpu.VMEM((NZ, BLOCKS, PIECE, R), jnp.bfloat16),
            pltpu.VMEM((2, NCH, BLOCKS, HALF, R), F32),
            pltpu.VMEM((2, 4, NCH, BLOCKS, CHUNK, R), F32),
            pltpu.VMEM((NF, SLOTS, PIECE, R), F32),
            pltpu.VMEM((BLOCKS, PIECE, R), F32),
            pltpu.VMEM((BLOCKS, PIECE, R), F32),
            pltpu.VMEM((NF, SLOTS, PIECE, R), F32),
            pltpu.VMEM((BLOCKS, R, R), F32),
            pltpu.VMEM((NF, R, R), F32),
            pltpu.VMEM((NF, CHUNK, R), F32),
            pltpu.VMEM((BLOCKS, R, R), F32),
            pltpu.SMEM((NF * SLOTS,), jnp.int32),
            pltpu.SMEM((NF * SLOTS,), F32),
            dma((NZ,)), dma((NZ,)), dma((NZ,)),
            dma((2, 4, NCH)), dma((2, 4, NCH)),
            dma, dma, dma, dma, dma, dma,
            dma((BLOCKS,)), dma, dma((BLOCKS,)), dma, dma, dma((BLOCKS,)),
        ],
        compiler_params=pltpu.CompilerParams(
            collective_id=0, has_side_effects=True, vmem_limit_bytes=48 * 2**20),
    )(raw, owner[:, 0], previous)
    renewed = RATE * previous + gathered
    return update, renewed[None, None]


def solution(mesh):
    return jax.shard_map(
        local,
        mesh=mesh,
        in_specs=(P("dp", None, "fsdp", None), P(), P("dp", "fsdp", None, None, None)),
        out_specs=(P("dp", "fsdp", None), P("dp", "fsdp", None, None, None)),
        check_vma=False,
    )
```

```python
import functools
import math

import jax
import jax.numpy as jnp
from jax import lax
from jax.experimental import pallas as pl
from jax.experimental.pallas import tpu as pltpu
from jax.sharding import PartitionSpec as P

MESH = pl.DeviceIdType.MESH
F32 = jnp.float32

NZ = 8
NA = 4
NF = NA * NA
BLOCKS = 8
SLOTS = 2
D = 2560
R = 128
PIECE = D // NF
CHUNK = 16
HALF = CHUNK // 2
NCH = PIECE // CHUNK
MID = PIECE // 2
EARLY_CH = 6
EARLY = EARLY_CH * CHUNK
LATE_CH = NCH - EARLY_CH
LEAD = 4
MERGE = 3
NEAR = 5
SPLIT = 16
PACKED = 72
ITERS = 3

COEF_A = 3.4445
COEF_B = -4.775
COEF_C = 2.0315
RATE = 0.95

OFFSETS = ((2, 2), (0, 2), (2, 0), (1, 2), (2, 1), (3, 2), (2, 3), (1, 1), (3, 3), (1, 3), (3, 1), (0, 1), (1, 0), (0, 3), (3, 0))
ORDER = (4, 3, 5, 2, 6, 1, 7, 0)
RIGHT, LEFT = 0, 1


def dot(a, b):
    return lax.dot_general(a, b, (((1,), (0,)), ((), ())), precision=lax.Precision.HIGHEST, preferred_element_type=F32)


def dot_t(a, b):
    return lax.dot_general(a, b, (((0,), (0,)), ((), ())), precision=lax.Precision.HIGHEST, preferred_element_type=F32)


def polynomial(gram):
    rows = lax.broadcasted_iota(jnp.int32, (R, R), 0)
    cols = lax.broadcasted_iota(jnp.int32, (R, R), 1)
    eye = jnp.where(rows == cols, 1.0, 0.0).astype(F32)
    total = jnp.sum(jnp.sum(gram * eye, axis=1, keepdims=True), axis=0, keepdims=True)
    inv = 1.0 / (jnp.sqrt(total) + 1e-07)
    gram = (gram * inv) * inv
    product = None
    for sweep in range(ITERS):
        poly = COEF_A * eye + COEF_B * gram + COEF_C * dot(gram, gram)
        product = poly if product is None else dot(product, poly)
        if sweep < ITERS - 1:
            gram = dot(poly, dot(gram, poly))
    return (0.2 * math.sqrt(D)) * inv * product


def pack(matrix):
    rows = lax.broadcasted_iota(jnp.int32, (R // 2, R), 0)
    cols = lax.broadcasted_iota(jnp.int32, (R // 2, R), 1)
    top, bottom = matrix[:R // 2], matrix[R // 2:]
    body = jnp.where(rows > cols, pltpu.roll(bottom, R // 2, 1), top)
    diagonal = jnp.sum(jnp.where(rows == cols - R // 2, bottom, 0.0), axis=0, keepdims=True)
    return body, jnp.broadcast_to(diagonal, (PACKED - R // 2, R))


def unpack(body, diagonal):
    rows = lax.broadcasted_iota(jnp.int32, (R // 2, R), 0)
    cols = lax.broadcasted_iota(jnp.int32, (R // 2, R), 1)
    turned = jnp.concatenate([body, jnp.zeros_like(body)], axis=0).T
    left = turned[:R // 2]
    top = jnp.where(rows <= cols, body, left)
    last = jnp.where(rows > cols - R // 2, pltpu.roll(body, R // 2, 1), pltpu.roll(left, R // 2, 1))
    last = jnp.where(rows == cols - R // 2, diagonal, last)
    bottom = jnp.where(cols < R // 2, turned[R // 2:], last)
    return jnp.concatenate([top, bottom], axis=0)


def remote(src, dst, send, recv, to):
    return pltpu.make_async_remote_copy(
        src_ref=src, dst_ref=dst, send_sem=send, recv_sem=recv, device_id=to, device_id_type=MESH)


def kernel(
    grads, owner, mom, update, renewed,
    who, raw, sib, r0, rz, momv, m1, m2s, m2r, m3s, m3r, gbuf, vbuf, gx, gr, gsend, grecv, rrecv, qbuf, idx_tab, val_tab,
    who_sem, raw_sem, mom_sem, sib_s, sib_r, t0_s, t0_r, z_s, z_r, m1_s, m1_r, m1_l, m2_ss, m2_rs, m3_ss, m3_rs,
    gx_s, gx_r, p_s, p_r, l_s, l_r, q_s, q_r,
):
    group = lax.axis_index("dp")
    f = lax.axis_index("fsdp")
    z, c = group // 2, group % 2
    me = (f // NA, f % NA)

    def z_of(step):
        return (z + step) % NZ

    def z_dev(d, core):
        return (z_of(1 if d == RIGHT else NZ - 1) * 2 + core, f)

    def plane(dy, dx):
        return ((me[0] + dy) % NA) * NA + (me[1] + dx) % NA

    def along(axis, step):
        return (group, plane(step, 0) if axis == 0 else plane(0, step))

    def on(axis, step):
        return (me[axis] + step) % NA

    def chunk(k):
        return pl.ds(pl.multiple_of(k * CHUNK, CHUNK), CHUNK)

    sibling = (z * 2 + 1 - c, f)

    who_copy = pltpu.make_async_copy(owner, who, who_sem)
    who_copy.start()
    raw_copy = [pltpu.make_async_copy(grads.at[z_of(j)], raw.at[z_of(j)], raw_sem.at[j]) for j in range(NZ)]
    for j in ORDER:
        raw_copy[j].start()
    mom_copy = pltpu.make_async_copy(mom, momv, mom_sem)
    mom_copy.start()

    barrier = pltpu.get_barrier_semaphore()
    peers = (sibling,) + tuple(z_dev(d, core) for d in (RIGHT, LEFT) for core in (c, 1 - c))
    peers += tuple((group, plane(dy, dx)) for dy, dx in OFFSETS)
    for peer in peers:
        pl.semaphore_signal(barrier, inc=1, device_id=peer, device_id_type=MESH)

    who_copy.wait()
    owners = [who[group * BLOCKS + m] for m in range(BLOCKS)]
    owner_at = ([lax.shift_right_logical(o, 2) for o in owners], [jnp.bitwise_and(o, 3) for o in owners])
    places = []
    for m in range(BLOCKS):
        place = jnp.int32(0)
        for earlier in range(m):
            place = place + jnp.where(owners[earlier] == owners[m], 1, 0).astype(jnp.int32)
        places.append(jnp.minimum(place, SLOTS - 1))
    keys = [owners[m] * SLOTS + places[m] for m in range(BLOCKS)]

    def table(slot, carry):
        index, valid = jnp.int32(0), jnp.float32(0)
        for m in range(BLOCKS):
            hit = keys[m] == slot
            index = jnp.where(hit, m, index)
            valid = jnp.where(hit, 1.0, valid)
        idx_tab[slot] = index
        val_tab[slot] = valid
        return carry

    lax.fori_loop(0, NF * SLOTS, table, 0)

    pl.semaphore_wait(barrier, len(peers))

    def t0_copies(k, q):
        return [
            remote(raw.at[z_of(4), core, :, chunk(k)], r0.at[k, i], t0_s.at[k, i], t0_r.at[k, i], z_dev(q, core))
            for i, core in enumerate((c, 1 - c))
        ]

    def z_copy(d, t, k):
        return remote(rz.at[d, t - 1, k], rz.at[d, t, k], z_s.at[d, t - 1, k], z_r.at[d, t - 1, k], z_dev(d, c))

    sib_copy = [
        None if j == 4 else remote(raw.at[z_of(j), 1 - c], sib.at[z_of(j)], sib_s.at[j], sib_r.at[j], sibling)
        for j in range(NZ)
    ]

    raw_copy[4].wait()
    for k in range(LEAD):
        for copy in t0_copies(k, k % 2):
            copy.start()
    for j in ORDER[1:]:
        raw_copy[j].wait()
        sib_copy[j].start()

    def m1_copy(h, j, first=0, count=MID):
        to = on(h, j)
        if h == 0:
            src = momv.at[:, to, :, pl.ds(first, count)]
        else:
            src = momv.at[:, :, to, pl.ds(MID + first, count)]
        dst = m1.at[h, me[h], :, :, pl.ds(first, count)]
        return remote(src, dst, m1_s.at[h, j - 1], m1_r.at[h, j - 1], along(h, j))

    def m1_local(h):
        if h == 0:
            src = momv.at[:, me[0], :, pl.ds(0, MID)]
        else:
            src = momv.at[:, :, me[1], pl.ds(MID, MID)]
        return pltpu.make_async_copy(src, m1.at[h, me[h]], m1_l.at[h])

    mom_copy.wait()
    for first in range(0, MID, SPLIT):
        for j in (2, 1, 3):
            for h in range(2):
                m1_copy(h, j, first, SPLIT).start()
    for h in range(2):
        m1_local(h).start()

    def held(h, step, m, first, count):
        b = 1 - h
        keep = jnp.where(owner_at[b][m] == me[b], 1.0, 0.0).astype(F32)
        return m1[h, owner_at[h][m], places[m], on(b, step), first:first + count, :] * keep

    def m2_copy(h, d):
        return remote(m2s.at[h, d], m2r.at[h, d], m2_ss.at[h, d], m2_rs.at[h, d], along(1 - h, 1 if d == RIGHT else 3))

    def m3_copy(h, d):
        return remote(m3s.at[h, d], m3r.at[h, d], m3_ss.at[h, d], m3_rs.at[h, d], along(1 - h, 1 if d == RIGHT else 3))

    QUARTER = MID // 2

    def merge_far():
        for h in range(2):
            for j in (1, 2, 3):
                m1_copy(h, j).wait_recv()
            m1_local(h).wait()
        for h in range(2):
            for d in (RIGHT, LEFT):
                for m in range(BLOCKS):
                    m2s[h, d, m] = held(h, 2, m, QUARTER * d, QUARTER)
                m2_copy(h, d).start()

    def merge_near():
        for h in range(2):
            for d in (RIGHT, LEFT):
                step = 1 if d == RIGHT else 3
                for m in range(BLOCKS):
                    m3s[h, d, m] = held(h, step, m, 0, MID)
                m2_copy(h, d).wait_recv()
                m3s[h, d, :, QUARTER * d:QUARTER * d + QUARTER, :] += m2r[h, d]
                m3_copy(h, d).start()

    def pair_sum(at, k):
        return raw[at, c, :, chunk(k), :].astype(F32) + sib[at, :, chunk(k), :].astype(F32)

    def hop(t, k, q):
        for d in (RIGHT, LEFT):
            step = 4 - t if d == RIGHT else NZ - 4 + t

            @pl.when(k == 0)
            def _():
                sib_copy[step].wait_recv()

            at = z_of(step)
            if t > 1:
                z_copy(d, t - 1, k).wait_recv()
                rz[d, t - 1, k] += pair_sum(at, k)
            elif d == q:
                for copy in t0_copies(k, q):
                    copy.wait_recv()
                rz[d, 0, k] = pair_sum(at, k) + (r0[k, 0].astype(F32) + r0[k, 1].astype(F32))
            else:
                rz[d, 0, k] = pair_sum(at, k)
            z_copy(d, t, k).start()

    def finish(k):
        z_copy(RIGHT, 3, k).wait_recv()
        z_copy(LEFT, 3, k).wait_recv()
        gbuf[:, chunk(k), :] = (pair_sum(z, k) + rz[RIGHT, 3, k] + rz[LEFT, 3, k]) * (1.0 / 16.0)

    def direct(pair):
        rows = pl.ds(pl.multiple_of(pair * 2 * CHUNK, 2 * CHUNK), 2 * CHUNK)

        def fill(to, carry):
            for s in range(SLOTS):
                gx[pair, to, s] = gbuf[idx_tab[to * SLOTS + s], rows, :] * val_tab[to * SLOTS + s]
            return carry

        lax.fori_loop(0, NF, fill, 0)
        for dy, dx in OFFSETS:
            to = plane(dy, dx)
            remote(gx.at[pair, to], gr.at[:, me[0], me[1], rows], gx_s, gx_r, (group, to)).start()
        gr[:, me[0], me[1], rows, :] = gx[pair, f]

    def velocity(first, count):
        for h in range(2):
            low, high = max(first, h * MID), min(first + count, (h + 1) * MID)
            if low >= high:
                continue
            at, n = low - h * MID, high - low
            for m in range(BLOCKS):
                state = held(h, 0, m, at, n) + m3r[h, RIGHT, m, at:at + n, :] + m3r[h, LEFT, m, at:at + n, :]
                vbuf[m, low:high, :] = (1.0 + RATE) * gbuf[m, low:high, :] + (RATE * RATE) * state

    def handler(b):
        return 2 * b + c

    def gram_copy(b):
        return remote(gsend.at[b], grecv.at[f], p_s.at[b], p_r, (group, handler(b)))

    def late_copy(i, b):
        rows = pl.ds(EARLY + i * CHUNK, CHUNK)
        return remote(vbuf.at[b, rows], rrecv.at[i, f], l_s.at[i, b], l_r.at[i], (group, handler(b)))

    def send_gram():
        for h in range(2):
            for d in (RIGHT, LEFT):
                m3_copy(h, d).wait_recv()
        velocity(0, EARLY)
        for b in range(BLOCKS):
            part = vbuf[b, 0:EARLY, :]
            body, diagonal = pack(dot_t(part, part))
            gsend[b, 0:R // 2, :] = body
            gsend[b, R // 2:PACKED, :] = diagonal

            @pl.when(handler(b) != f)
            def _():
                gram_copy(b).start()

    def send_late(i):
        velocity(EARLY + i * CHUNK, CHUNK)
        for b in range(BLOCKS):
            @pl.when(handler(b) != f)
            def _():
                late_copy(i, b).start()

    def when(k, run, low=0, high=NCH):
        @pl.when((k >= low) & (k < high))
        def _():
            run(k)

    def slots(sp, carry):
        for q in range(2):
            s = sp * 2 + q
            other = 1 - q
            when(s, lambda k: hop(1, k, q))
            when(s - 1, lambda k: hop(2, k, other))
            when(s - 2, lambda k: hop(3, k, q))

            @pl.when(s + LEAD < NCH)
            def _():
                for copy in t0_copies(s + LEAD, q):
                    copy.start()

            @pl.when(s == 3)
            def _():
                sib_copy[0].wait_recv()

            when(s - 3, finish)
            if q == 0:
                when(s - 4, lambda k: direct(k // 2), 0, NCH - 2)
            for at, run in (
                (MERGE, merge_far), (NEAR, merge_near), (2 + EARLY_CH, send_gram),
            ) + tuple((3 + EARLY_CH + i, functools.partial(send_late, i)) for i in range(LATE_CH - 1)):
                if at % 2 == q:
                    @pl.when(s == at)
                    def _():
                        run()
        return carry

    lax.fori_loop(0, (NCH + 2) // 2, slots, 0)

    last = NCH - 1
    finish(last)
    send_late(LATE_CH - 1)
    direct(NCH // 2 - 1)

    mine = f // 2
    handles = f % 2 == c

    def q_copy(to):
        return remote(qbuf.at[mine], qbuf.at[mine], q_s, q_r.at[mine], (group, to))

    @pl.when(handles)
    def _():
        grecv[f] = gsend[mine]
        for i in range(LATE_CH):
            rrecv[i, f] = vbuf[mine, EARLY + i * CHUNK:EARLY + (i + 1) * CHUNK, :]
        pltpu.make_async_copy(grecv.at[pl.ds(0, NF - 1)], grecv.at[pl.ds(0, NF - 1)], p_r).wait()
        total = grecv[0]
        for i in range(1, NF):
            total = total + grecv[i]
        gram = unpack(total[0:R // 2], total[R // 2:R // 2 + 1])
        for i in range(LATE_CH):
            pltpu.make_async_copy(rrecv.at[i, pl.ds(0, NF - 1)], rrecv.at[i, pl.ds(0, NF - 1)], l_r.at[i]).wait()
            late = rrecv[i].reshape(NF * CHUNK, R)
            gram = gram + dot_t(late, late)
        body, diagonal = pack(polynomial(gram))
        qbuf[mine, 0:R // 2, :] = body
        qbuf[mine, R // 2:PACKED, :] = diagonal
        for dy, dx in OFFSETS:
            q_copy(plane(dy, dx)).start()

    def receive_update():
        for b in range(BLOCKS):
            @pl.when(handler(b) != f)
            def _():
                pltpu.make_async_copy(qbuf.at[b], qbuf.at[b], q_r.at[b]).wait()

            update[b] = dot(vbuf[b], unpack(qbuf[b, 0:R // 2, :], qbuf[b, R // 2:R // 2 + 1, :]))

    def receive_gradient():
        part = gx.at[:, pl.ds(0, NF - 1)]
        pltpu.make_async_copy(part, part, gx_r).wait()
        for s in range(SLOTS):
            for a in range(NA):
                renewed[s, a] = RATE * momv[s, a] + gr[s, a]

    for b in range(BLOCKS):
        @pl.when(handler(b) != f)
        def _():
            gram_copy(b).wait_send()
            for i in range(LATE_CH):
                late_copy(i, b).wait_send()

    for j in ORDER[1:]:
        sib_copy[j].wait_send()
    for h in range(2):
        for j in (1, 2, 3):
            m1_copy(h, j).wait_send()
        for d in (RIGHT, LEFT):
            m2_copy(h, d).wait_send()
            m3_copy(h, d).wait_send()

    def drain(k, carry):
        for copy in t0_copies(k, 0):
            copy.wait_send()
        for d in (RIGHT, LEFT):
            for t in (1, 2, 3):
                z_copy(d, t, k).wait_send()
        return carry

    lax.fori_loop(0, NCH, drain, 0)
    receive_update()
    receive_gradient()

    @pl.when(handles)
    def _():
        part = grecv.at[pl.ds(0, NF - 1)]
        pltpu.make_async_copy(part, part, q_s).wait()

    part = gx.at[:, pl.ds(0, NF - 1)]
    pltpu.make_async_copy(part, part, gx_s).wait()


def place(update, renewed, update_out, renewed_out, sem):
    copies = (
        pltpu.make_async_copy(renewed, renewed_out, sem.at[0]),
        pltpu.make_async_copy(update, update_out, sem.at[1]),
    )
    for copy in copies:
        copy.start()
    for copy in copies:
        copy.wait()


def local(grads, owner, momentum):
    raw = grads[0].reshape(NZ, 2, BLOCKS, PIECE, R)
    previous = momentum[0, 0].reshape(SLOTS, NA, NA, PIECE, R)
    dma = pltpu.SemaphoreType.DMA

    def hbm(array):
        return pltpu.with_memory_space_constraint(array, pltpu.HBM)

    update, renewed = pl.pallas_call(
        kernel,
        out_shape=(
            pltpu.VMEM((BLOCKS, PIECE, R), F32),
            pltpu.VMEM((SLOTS, NA, NA, PIECE, R), F32),
        ),
        in_specs=[
            pl.BlockSpec(memory_space=pl.ANY),
            pl.BlockSpec(memory_space=pl.ANY),
            pl.BlockSpec(memory_space=pl.ANY),
        ],
        out_specs=(pl.BlockSpec(memory_space=pltpu.VMEM), pl.BlockSpec(memory_space=pltpu.VMEM)),
        scratch_shapes=[
            pltpu.SMEM((NF * BLOCKS,), jnp.int32),
            pltpu.VMEM((NZ, 2, BLOCKS, PIECE, R), jnp.bfloat16),
            pltpu.VMEM((NZ, BLOCKS, PIECE, R), jnp.bfloat16),
            pltpu.VMEM((NCH, 2, BLOCKS, CHUNK, R), jnp.bfloat16),
            pltpu.VMEM((2, 4, NCH, BLOCKS, CHUNK, R), F32),
            pltpu.VMEM((SLOTS, NA, NA, PIECE, R), F32),
            pltpu.VMEM((2, NA, SLOTS, NA, MID, R), F32),
            pltpu.VMEM((2, 2, BLOCKS, MID // 2, R), F32),
            pltpu.VMEM((2, 2, BLOCKS, MID // 2, R), F32),
            pltpu.VMEM((2, 2, BLOCKS, MID, R), F32),
            pltpu.VMEM((2, 2, BLOCKS, MID, R), F32),
            pltpu.VMEM((BLOCKS, PIECE, R), F32),
            pltpu.VMEM((BLOCKS, PIECE, R), F32),
            pltpu.VMEM((NCH // 2, NF, SLOTS, 2 * CHUNK, R), F32),
            pltpu.VMEM((SLOTS, NA, NA, PIECE, R), F32),
            pltpu.VMEM((BLOCKS, PACKED, R), F32),
            pltpu.VMEM((NF, PACKED, R), F32),
            pltpu.VMEM((LATE_CH, NF, CHUNK, R), F32),
            pltpu.VMEM((BLOCKS, PACKED, R), F32),
            pltpu.SMEM((NF * SLOTS,), jnp.int32),
            pltpu.SMEM((NF * SLOTS,), F32),
            dma, dma((NZ,)), dma, dma((NZ,)), dma((NZ,)),
            dma((NCH, 2)), dma((NCH, 2)), dma((2, 3, NCH)), dma((2, 3, NCH)),
            dma((2, 3)), dma((2, 3)), dma((2,)), dma((2, 2)), dma((2, 2)), dma((2, 2)), dma((2, 2)),
            dma, dma,
            dma((BLOCKS,)), dma, dma((LATE_CH, BLOCKS)), dma((LATE_CH,)), dma, dma((BLOCKS,)),
        ],
        compiler_params=pltpu.CompilerParams(
            collective_id=0, has_side_effects=True, vmem_limit_bytes=48 * 2**20),
    )(hbm(raw), hbm(owner[:, 0]), hbm(previous))
    update, renewed = pl.pallas_call(
        place,
        out_shape=(
            jax.ShapeDtypeStruct((BLOCKS, PIECE, R), F32),
            jax.ShapeDtypeStruct((SLOTS, NA, NA, PIECE, R), F32),
        ),
        in_specs=[pl.BlockSpec(memory_space=pl.ANY)] * 2,
        out_specs=(pl.BlockSpec(memory_space=pl.ANY),) * 2,
        scratch_shapes=[dma((2,))],
    )(pltpu.with_memory_space_constraint(update, pltpu.VMEM), pltpu.with_memory_space_constraint(renewed, pltpu.VMEM))
    return update, renewed.reshape(1, 1, SLOTS, D, R)


def solution(mesh):
    return jax.shard_map(
        local,
        mesh=mesh,
        in_specs=(P("dp", None, "fsdp", None), P(), P("dp", "fsdp", None, None, None)),
        out_specs=(P("dp", "fsdp", None), P("dp", "fsdp", None, None, None)),
        check_vma=False,
    )
```

```python
import functools
import math

import jax
import jax.numpy as jnp
from jax import lax
from jax.experimental import pallas as pl
from jax.experimental.pallas import tpu as pltpu
from jax.sharding import PartitionSpec as P

MESH = pl.DeviceIdType.MESH
F32 = jnp.float32

NZ = 8
NA = 4
NF = NA * NA
BLOCKS = 8
SLOTS = 2
D = 2560
R = 128
PIECE = D // NF
CHUNK = 16
HALF = CHUNK // 2
NCH = PIECE // CHUNK
MID = PIECE // 2
EARLY_CH = 6
EARLY = EARLY_CH * CHUNK
LATE_CH = NCH - EARLY_CH
LEAD = 4
MERGE = 3
NEAR = 5
SPLIT = 80
PACKED = 72
ITERS = 3

COEF_A = 3.4445
COEF_B = -4.775
COEF_C = 2.0315
RATE = 0.95

OFFSETS = ((2, 2), (0, 2), (2, 0), (1, 2), (2, 1), (3, 2), (2, 3), (1, 1), (3, 3), (1, 3), (3, 1), (0, 1), (1, 0), (0, 3), (3, 0))
ORDER = (4, 3, 5, 2, 6, 1, 7, 0)
RIGHT, LEFT = 0, 1


def dot(a, b):
    return lax.dot_general(a, b, (((1,), (0,)), ((), ())), precision=lax.Precision.HIGHEST, preferred_element_type=F32)


def dot_t(a, b):
    return lax.dot_general(a, b, (((0,), (0,)), ((), ())), precision=lax.Precision.HIGHEST, preferred_element_type=F32)


def polynomial(gram):
    rows = lax.broadcasted_iota(jnp.int32, (R, R), 0)
    cols = lax.broadcasted_iota(jnp.int32, (R, R), 1)
    eye = jnp.where(rows == cols, 1.0, 0.0).astype(F32)
    total = jnp.sum(jnp.sum(gram * eye, axis=1, keepdims=True), axis=0, keepdims=True)
    inv = 1.0 / (jnp.sqrt(total) + 1e-07)
    gram = (gram * inv) * inv
    product = None
    for sweep in range(ITERS):
        poly = COEF_A * eye + COEF_B * gram + COEF_C * dot(gram, gram)
        product = poly if product is None else dot(product, poly)
        if sweep < ITERS - 1:
            gram = dot(poly, dot(gram, poly))
    return (0.2 * math.sqrt(D)) * inv * product


def pack(matrix):
    rows = lax.broadcasted_iota(jnp.int32, (R // 2, R), 0)
    cols = lax.broadcasted_iota(jnp.int32, (R // 2, R), 1)
    top, bottom = matrix[:R // 2], matrix[R // 2:]
    body = jnp.where(rows > cols, pltpu.roll(bottom, R // 2, 1), top)
    diagonal = jnp.sum(jnp.where(rows == cols - R // 2, bottom, 0.0), axis=0, keepdims=True)
    return body, jnp.broadcast_to(diagonal, (PACKED - R // 2, R))


def unpack(body, diagonal):
    rows = lax.broadcasted_iota(jnp.int32, (R // 2, R), 0)
    cols = lax.broadcasted_iota(jnp.int32, (R // 2, R), 1)
    turned = jnp.concatenate([body, jnp.zeros_like(body)], axis=0).T
    left = turned[:R // 2]
    top = jnp.where(rows <= cols, body, left)
    last = jnp.where(rows > cols - R // 2, pltpu.roll(body, R // 2, 1), pltpu.roll(left, R // 2, 1))
    last = jnp.where(rows == cols - R // 2, diagonal, last)
    bottom = jnp.where(cols < R // 2, turned[R // 2:], last)
    return jnp.concatenate([top, bottom], axis=0)


def remote(src, dst, send, recv, to):
    return pltpu.make_async_remote_copy(
        src_ref=src, dst_ref=dst, send_sem=send, recv_sem=recv, device_id=to, device_id_type=MESH)


def kernel(
    grads, owner, mom, update, renewed,
    who, raw, sib, r0, rz, momv, m1, m2s, m2r, m3s, m3r, gbuf, vbuf, gx, gr, gsend, grecv, rrecv, qbuf, idx_tab, val_tab,
    who_sem, raw_sem, mom_sem, sib_s, sib_r, t0_s, t0_r, z_s, z_r, m1_s, m1_r, m1_l, m2_ss, m2_rs, m3_ss, m3_rs,
    gx_s, gx_r, p_s, p_r, l_s, l_r, q_s, q_r,
):
    group = lax.axis_index("dp")
    f = lax.axis_index("fsdp")
    z, c = group // 2, group % 2
    me = (f // NA, f % NA)

    def z_of(step):
        return (z + step) % NZ

    def z_dev(d, core):
        return (z_of(1 if d == RIGHT else NZ - 1) * 2 + core, f)

    def plane(dy, dx):
        return ((me[0] + dy) % NA) * NA + (me[1] + dx) % NA

    def along(axis, step):
        return (group, plane(step, 0) if axis == 0 else plane(0, step))

    def on(axis, step):
        return (me[axis] + step) % NA

    def chunk(k):
        return pl.ds(pl.multiple_of(k * CHUNK, CHUNK), CHUNK)

    sibling = (z * 2 + 1 - c, f)

    who_copy = pltpu.make_async_copy(owner, who, who_sem)
    who_copy.start()
    raw_copy = [pltpu.make_async_copy(grads.at[z_of(j)], raw.at[z_of(j)], raw_sem.at[j]) for j in range(NZ)]
    for j in ORDER:
        raw_copy[j].start()
    mom_copy = pltpu.make_async_copy(mom, momv, mom_sem)
    mom_copy.start()

    barrier = pltpu.get_barrier_semaphore()
    peers = (sibling,) + tuple(z_dev(d, core) for d in (RIGHT, LEFT) for core in (c, 1 - c))
    peers += tuple((group, plane(dy, dx)) for dy, dx in OFFSETS)
    for peer in peers:
        pl.semaphore_signal(barrier, inc=1, device_id=peer, device_id_type=MESH)

    pl.semaphore_wait(barrier, len(peers))

    def t0_copies(k, q):
        return [
            remote(raw.at[z_of(4), core, :, chunk(k)], r0.at[k, i], t0_s.at[k, i], t0_r.at[k, i], z_dev(q, core))
            for i, core in enumerate((c, 1 - c))
        ]

    def z_copy(d, t, k):
        return remote(rz.at[d, t - 1, k], rz.at[d, t, k], z_s.at[d, t - 1, k], z_r.at[d, t - 1, k], z_dev(d, c))

    sib_copy = [
        None if j == 4 else remote(raw.at[z_of(j), 1 - c], sib.at[z_of(j)], sib_s.at[j], sib_r.at[j], sibling)
        for j in range(NZ)
    ]

    raw_copy[4].wait()
    for k in range(LEAD):
        for copy in t0_copies(k, k % 2):
            copy.start()
    for j in ORDER[1:]:
        raw_copy[j].wait()
        sib_copy[j].start()

    def m1_copy(h, j, first=0, count=MID):
        to = on(h, j)
        if h == 0:
            src = momv.at[:, to, :, pl.ds(first, count)]
        else:
            src = momv.at[:, :, to, pl.ds(MID + first, count)]
        dst = m1.at[h, me[h], :, :, pl.ds(first, count)]
        return remote(src, dst, m1_s.at[h, j - 1], m1_r.at[h, j - 1], along(h, j))

    def m1_local(h):
        if h == 0:
            src = momv.at[:, me[0], :, pl.ds(0, MID)]
        else:
            src = momv.at[:, :, me[1], pl.ds(MID, MID)]
        return pltpu.make_async_copy(src, m1.at[h, me[h]], m1_l.at[h])

    mom_copy.wait()
    for first in range(0, MID, SPLIT):
        for j in (2, 1, 3):
            for h in range(2):
                m1_copy(h, j, first, SPLIT).start()
    for h in range(2):
        m1_local(h).start()

    who_copy.wait()
    owners = [who[group * BLOCKS + m] for m in range(BLOCKS)]
    owner_at = ([lax.shift_right_logical(o, 2) for o in owners], [jnp.bitwise_and(o, 3) for o in owners])
    places = []
    for m in range(BLOCKS):
        place = jnp.int32(0)
        for earlier in range(m):
            place = place + jnp.where(owners[earlier] == owners[m], 1, 0).astype(jnp.int32)
        places.append(jnp.minimum(place, SLOTS - 1))
    keys = [owners[m] * SLOTS + places[m] for m in range(BLOCKS)]

    def table(slot, carry):
        index, valid = jnp.int32(0), jnp.float32(0)
        for m in range(BLOCKS):
            hit = keys[m] == slot
            index = jnp.where(hit, m, index)
            valid = jnp.where(hit, 1.0, valid)
        idx_tab[slot] = index
        val_tab[slot] = valid
        return carry

    lax.fori_loop(0, NF * SLOTS, table, 0)

    def held(h, step, m, first, count):
        b = 1 - h
        keep = jnp.where(owner_at[b][m] == me[b], 1.0, 0.0).astype(F32)
        return m1[h, owner_at[h][m], places[m], on(b, step), first:first + count, :] * keep

    def m2_copy(h, d):
        return remote(m2s.at[h, d], m2r.at[h, d], m2_ss.at[h, d], m2_rs.at[h, d], along(1 - h, 1 if d == RIGHT else 3))

    def m3_copy(h, d):
        return remote(m3s.at[h, d], m3r.at[h, d], m3_ss.at[h, d], m3_rs.at[h, d], along(1 - h, 1 if d == RIGHT else 3))

    QUARTER = MID // 2

    def merge_far():
        for h in range(2):
            for j in (1, 2, 3):
                m1_copy(h, j).wait_recv()
            m1_local(h).wait()
        for h in range(2):
            for d in (RIGHT, LEFT):
                for m in range(BLOCKS):
                    m2s[h, d, m] = held(h, 2, m, QUARTER * d, QUARTER)
                m2_copy(h, d).start()

    def merge_near():
        for h in range(2):
            for d in (RIGHT, LEFT):
                step = 1 if d == RIGHT else 3
                for m in range(BLOCKS):
                    m3s[h, d, m] = held(h, step, m, 0, MID)
                m2_copy(h, d).wait_recv()
                m3s[h, d, :, QUARTER * d:QUARTER * d + QUARTER, :] += m2r[h, d]
                m3_copy(h, d).start()

    def pair_sum(at, k):
        return raw[at, c, :, chunk(k), :].astype(F32) + sib[at, :, chunk(k), :].astype(F32)

    def hop(t, k, q):
        for d in (RIGHT, LEFT):
            step = 4 - t if d == RIGHT else NZ - 4 + t

            @pl.when(k == 0)
            def _():
                sib_copy[step].wait_recv()

            at = z_of(step)
            if t > 1:
                z_copy(d, t - 1, k).wait_recv()
                rz[d, t - 1, k] += pair_sum(at, k)
            elif d == q:
                for copy in t0_copies(k, q):
                    copy.wait_recv()
                rz[d, 0, k] = pair_sum(at, k) + (r0[k, 0].astype(F32) + r0[k, 1].astype(F32))
            else:
                rz[d, 0, k] = pair_sum(at, k)
            z_copy(d, t, k).start()

    def finish(k):
        z_copy(RIGHT, 3, k).wait_recv()
        z_copy(LEFT, 3, k).wait_recv()
        gbuf[:, chunk(k), :] = (pair_sum(z, k) + rz[RIGHT, 3, k] + rz[LEFT, 3, k]) * (1.0 / 16.0)

    def direct(first, count):
        rows = pl.ds(pl.multiple_of(first, CHUNK), count)

        def fill(to, carry):
            for s in range(SLOTS):
                gx[to, s, rows, :] = gbuf[idx_tab[to * SLOTS + s], rows, :] * val_tab[to * SLOTS + s]
            return carry

        lax.fori_loop(0, NF, fill, 0)
        for dy, dx in OFFSETS:
            to = plane(dy, dx)
            remote(gx.at[to, :, rows], gr.at[:, me[0], me[1], rows], gx_s, gx_r, (group, to)).start()
        gr[:, me[0], me[1], rows, :] = gx[f, :, rows, :]

    def velocity(first, count):
        for h in range(2):
            low, high = max(first, h * MID), min(first + count, (h + 1) * MID)
            if low >= high:
                continue
            at, n = low - h * MID, high - low
            for m in range(BLOCKS):
                state = held(h, 0, m, at, n) + m3r[h, RIGHT, m, at:at + n, :] + m3r[h, LEFT, m, at:at + n, :]
                vbuf[m, low:high, :] = (1.0 + RATE) * gbuf[m, low:high, :] + (RATE * RATE) * state

    def handler(b):
        return 2 * b + c

    def gram_copy(b):
        return remote(gsend.at[b], grecv.at[f], p_s.at[b], p_r, (group, handler(b)))

    def late_copy(i, b):
        rows = pl.ds(EARLY + i * CHUNK, CHUNK)
        return remote(vbuf.at[b, rows], rrecv.at[i, f], l_s.at[i, b], l_r.at[i], (group, handler(b)))

    def send_gram():
        for h in range(2):
            for d in (RIGHT, LEFT):
                m3_copy(h, d).wait_recv()
        velocity(0, EARLY)
        for b in range(BLOCKS):
            part = vbuf[b, 0:EARLY, :]
            body, diagonal = pack(dot_t(part, part))
            gsend[b, 0:R // 2, :] = body
            gsend[b, R // 2:PACKED, :] = diagonal

            @pl.when(handler(b) != f)
            def _():
                gram_copy(b).start()

    def send_late(i):
        velocity(EARLY + i * CHUNK, CHUNK)
        for b in range(BLOCKS):
            @pl.when(handler(b) != f)
            def _():
                late_copy(i, b).start()

    def when(k, run, low=0, high=NCH):
        @pl.when((k >= low) & (k < high))
        def _():
            run(k)

    last = NCH - 1

    def slots(sp, carry):
        for q in range(2):
            s = sp * 2 + q
            other = 1 - q
            when(s, lambda k: hop(1, k, q))
            when(s - 1, lambda k: hop(2, k, other))
            when(s - 2, lambda k: hop(3, k, q))

            @pl.when(s + LEAD < NCH)
            def _():
                for copy in t0_copies(s + LEAD, q):
                    copy.start()

            @pl.when(s == 3)
            def _():
                sib_copy[0].wait_recv()

            when(s - 3, finish)
            if q == 0:
                when(s - 4, lambda k: direct(k * CHUNK, 2 * CHUNK), 0, NCH - 2)
            for at, run in (
                (MERGE, merge_far), (NEAR, merge_near), (2 + EARLY_CH, send_gram),
            ) + tuple((3 + EARLY_CH + i, functools.partial(send_late, i)) for i in range(LATE_CH - 1)):
                if at % 2 == q:
                    @pl.when(s == at)
                    def _():
                        run()
        return carry

    lax.fori_loop(0, (NCH + 2) // 2, slots, 0)

    finish(last)
    send_late(LATE_CH - 1)
    direct((last - 1) * CHUNK, CHUNK)

    mine = f // 2
    handles = f % 2 == c

    def q_copy(to):
        return remote(qbuf.at[mine], qbuf.at[mine], q_s, q_r.at[mine], (group, to))

    @pl.when(handles)
    def _():
        grecv[f] = gsend[mine]
        for i in range(LATE_CH):
            rrecv[i, f] = vbuf[mine, EARLY + i * CHUNK:EARLY + (i + 1) * CHUNK, :]
        pltpu.make_async_copy(grecv.at[pl.ds(0, NF - 1)], grecv.at[pl.ds(0, NF - 1)], p_r).wait()
        total = grecv[0]
        for i in range(1, NF):
            total = total + grecv[i]
        gram = unpack(total[0:R // 2], total[R // 2:R // 2 + 1])
        for i in range(LATE_CH):
            pltpu.make_async_copy(rrecv.at[i, pl.ds(0, NF - 1)], rrecv.at[i, pl.ds(0, NF - 1)], l_r.at[i]).wait()
            late = rrecv[i].reshape(NF * CHUNK, R)
            gram = gram + dot_t(late, late)
        body, diagonal = pack(polynomial(gram))
        qbuf[mine, 0:R // 2, :] = body
        qbuf[mine, R // 2:PACKED, :] = diagonal
        for dy, dx in OFFSETS:
            q_copy(plane(dy, dx)).start()

    def receive_update():
        for b in range(BLOCKS):
            @pl.when(handler(b) != f)
            def _():
                pltpu.make_async_copy(qbuf.at[b], qbuf.at[b], q_r.at[b]).wait()

            update[b] = dot(vbuf[b], unpack(qbuf[b, 0:R // 2, :], qbuf[b, R // 2:R // 2 + 1, :]))

    def receive_gradient():
        part = gx.at[pl.ds(0, NF - 1)]
        pltpu.make_async_copy(part, part, gx_r).wait()
        for s in range(SLOTS):
            for a in range(NA):
                renewed[s, a] = RATE * momv[s, a] + gr[s, a]

    for b in range(BLOCKS):
        @pl.when(handler(b) != f)
        def _():
            gram_copy(b).wait_send()
            for i in range(LATE_CH):
                late_copy(i, b).wait_send()

    for j in ORDER[1:]:
        sib_copy[j].wait_send()
    for h in range(2):
        for j in (1, 2, 3):
            m1_copy(h, j).wait_send()
        for d in (RIGHT, LEFT):
            m2_copy(h, d).wait_send()
            m3_copy(h, d).wait_send()

    def drain(k, carry):
        for copy in t0_copies(k, 0):
            copy.wait_send()
        for d in (RIGHT, LEFT):
            for t in (1, 2, 3):
                z_copy(d, t, k).wait_send()
        return carry

    lax.fori_loop(0, NCH, drain, 0)
    direct(last * CHUNK, CHUNK)
    receive_update()
    receive_gradient()

    @pl.when(handles)
    def _():
        part = grecv.at[pl.ds(0, NF - 1)]
        pltpu.make_async_copy(part, part, q_s).wait()

    part = gx.at[pl.ds(0, NF - 1)]
    pltpu.make_async_copy(part, part, gx_s).wait()


def place(update, renewed, update_out, renewed_out, sem):
    copies = []
    for i in range(BLOCKS):
        copies.append(pltpu.make_async_copy(renewed.at[i // 4, i % 4], renewed_out.at[i // 4, i % 4], sem.at[i]))
    for i in range(2):
        half = pl.ds(i * (BLOCKS // 2), BLOCKS // 2)
        copies.append(pltpu.make_async_copy(update.at[half], update_out.at[half], sem.at[BLOCKS + i]))
    for copy in copies:
        copy.start()
    for copy in copies:
        copy.wait()


def local(grads, owner, momentum):
    raw = grads[0].reshape(NZ, 2, BLOCKS, PIECE, R)
    previous = momentum[0, 0].reshape(SLOTS, NA, NA, PIECE, R)
    dma = pltpu.SemaphoreType.DMA

    def hbm(array):
        return pltpu.with_memory_space_constraint(array, pltpu.HBM)

    update, renewed = pl.pallas_call(
        kernel,
        out_shape=(
            pltpu.VMEM((BLOCKS, PIECE, R), F32),
            pltpu.VMEM((SLOTS, NA, NA, PIECE, R), F32),
        ),
        in_specs=[
            pl.BlockSpec(memory_space=pl.ANY),
            pl.BlockSpec(memory_space=pl.ANY),
            pl.BlockSpec(memory_space=pl.ANY),
        ],
        out_specs=(pl.BlockSpec(memory_space=pltpu.VMEM), pl.BlockSpec(memory_space=pltpu.VMEM)),
        scratch_shapes=[
            pltpu.SMEM((NF * BLOCKS,), jnp.int32),
            pltpu.VMEM((NZ, 2, BLOCKS, PIECE, R), jnp.bfloat16),
            pltpu.VMEM((NZ, BLOCKS, PIECE, R), jnp.bfloat16),
            pltpu.VMEM((NCH, 2, BLOCKS, CHUNK, R), jnp.bfloat16),
            pltpu.VMEM((2, 4, NCH, BLOCKS, CHUNK, R), F32),
            pltpu.VMEM((SLOTS, NA, NA, PIECE, R), F32),
            pltpu.VMEM((2, NA, SLOTS, NA, MID, R), F32),
            pltpu.VMEM((2, 2, BLOCKS, MID // 2, R), F32),
            pltpu.VMEM((2, 2, BLOCKS, MID // 2, R), F32),
            pltpu.VMEM((2, 2, BLOCKS, MID, R), F32),
            pltpu.VMEM((2, 2, BLOCKS, MID, R), F32),
            pltpu.VMEM((BLOCKS, PIECE, R), F32),
            pltpu.VMEM((BLOCKS, PIECE, R), F32),
            pltpu.VMEM((NF, SLOTS, PIECE, R), F32),
            pltpu.VMEM((SLOTS, NA, NA, PIECE, R), F32),
            pltpu.VMEM((BLOCKS, PACKED, R), F32),
            pltpu.VMEM((NF, PACKED, R), F32),
            pltpu.VMEM((LATE_CH, NF, CHUNK, R), F32),
            pltpu.VMEM((BLOCKS, PACKED, R), F32),
            pltpu.SMEM((NF * SLOTS,), jnp.int32),
            pltpu.SMEM((NF * SLOTS,), F32),
            dma, dma((NZ,)), dma, dma((NZ,)), dma((NZ,)),
            dma((NCH, 2)), dma((NCH, 2)), dma((2, 3, NCH)), dma((2, 3, NCH)),
            dma((2, 3)), dma((2, 3)), dma((2,)), dma((2, 2)), dma((2, 2)), dma((2, 2)), dma((2, 2)),
            dma, dma,
            dma((BLOCKS,)), dma, dma((LATE_CH, BLOCKS)), dma((LATE_CH,)), dma, dma((BLOCKS,)),
        ],
        compiler_params=pltpu.CompilerParams(
            collective_id=0, has_side_effects=True, vmem_limit_bytes=48 * 2**20),
    )(hbm(raw), hbm(owner[:, 0]), hbm(previous))
    update, renewed = pl.pallas_call(
        place,
        out_shape=(
            jax.ShapeDtypeStruct((BLOCKS, PIECE, R), F32),
            jax.ShapeDtypeStruct((SLOTS, NA, NA, PIECE, R), F32),
        ),
        in_specs=[pl.BlockSpec(memory_space=pl.ANY)] * 2,
        out_specs=(pl.BlockSpec(memory_space=pl.ANY),) * 2,
        scratch_shapes=[dma((BLOCKS + 2,))],
    )(pltpu.with_memory_space_constraint(update, pltpu.VMEM), pltpu.with_memory_space_constraint(renewed, pltpu.VMEM))
    return update, renewed.reshape(1, 1, SLOTS, D, R)


def solution(mesh):
    return jax.shard_map(
        local,
        mesh=mesh,
        in_specs=(P("dp", None, "fsdp", None), P(), P("dp", "fsdp", None, None, None)),
        out_specs=(P("dp", "fsdp", None), P("dp", "fsdp", None, None, None)),
        check_vma=False,
    )
```

```python
import functools
import math

import jax
import jax.numpy as jnp
from jax import lax
from jax.experimental import pallas as pl
from jax.experimental.pallas import tpu as pltpu
from jax.sharding import PartitionSpec as P

MESH = pl.DeviceIdType.MESH
F32 = jnp.float32

NZ = 8
NA = 4
NF = NA * NA
BLOCKS = 8
SLOTS = 2
D = 2560
R = 128
PIECE = D // NF
CHUNK = 16
HALF = CHUNK // 2
NCH = PIECE // CHUNK
MID = PIECE // 2
EARLY_CH = 6
EARLY = EARLY_CH * CHUNK
LATE_CH = NCH - EARLY_CH
LEAD = 4
MERGE = 3
NEAR = 5
SPLIT = 80
PACKED = 72
ITERS = 3

COEF_A = 3.4445
COEF_B = -4.775
COEF_C = 2.0315
RATE = 0.95

OFFSETS = ((2, 2), (0, 2), (2, 0), (1, 2), (2, 1), (3, 2), (2, 3), (1, 1), (3, 3), (1, 3), (3, 1), (0, 1), (1, 0), (0, 3), (3, 0))
ORDER = (4, 3, 5, 2, 6, 1, 7, 0)
RIGHT, LEFT = 0, 1


def dot(a, b):
    return lax.dot_general(a, b, (((1,), (0,)), ((), ())), precision=lax.Precision.HIGHEST, preferred_element_type=F32)


def dot_t(a, b):
    return lax.dot_general(a, b, (((0,), (0,)), ((), ())), precision=lax.Precision.HIGHEST, preferred_element_type=F32)


def polynomial(gram):
    rows = lax.broadcasted_iota(jnp.int32, (R, R), 0)
    cols = lax.broadcasted_iota(jnp.int32, (R, R), 1)
    eye = jnp.where(rows == cols, 1.0, 0.0).astype(F32)
    total = jnp.sum(jnp.sum(gram * eye, axis=1, keepdims=True), axis=0, keepdims=True)
    inv = 1.0 / (jnp.sqrt(total) + 1e-07)
    gram = (gram * inv) * inv
    product = None
    for sweep in range(ITERS):
        poly = COEF_A * eye + COEF_B * gram + COEF_C * dot(gram, gram)
        product = poly if product is None else dot(product, poly)
        if sweep < ITERS - 1:
            gram = dot(poly, dot(gram, poly))
    return (0.2 * math.sqrt(D)) * inv * product


def pack(matrix):
    rows = lax.broadcasted_iota(jnp.int32, (R // 2, R), 0)
    cols = lax.broadcasted_iota(jnp.int32, (R // 2, R), 1)
    top, bottom = matrix[:R // 2], matrix[R // 2:]
    body = jnp.where(rows > cols, pltpu.roll(bottom, R // 2, 1), top)
    diagonal = jnp.sum(jnp.where(rows == cols - R // 2, bottom, 0.0), axis=0, keepdims=True)
    return body, jnp.broadcast_to(diagonal, (PACKED - R // 2, R))


def unpack(body, diagonal):
    rows = lax.broadcasted_iota(jnp.int32, (R // 2, R), 0)
    cols = lax.broadcasted_iota(jnp.int32, (R // 2, R), 1)
    turned = jnp.concatenate([body, jnp.zeros_like(body)], axis=0).T
    left = turned[:R // 2]
    top = jnp.where(rows <= cols, body, left)
    last = jnp.where(rows > cols - R // 2, pltpu.roll(body, R // 2, 1), pltpu.roll(left, R // 2, 1))
    last = jnp.where(rows == cols - R // 2, diagonal, last)
    bottom = jnp.where(cols < R // 2, turned[R // 2:], last)
    return jnp.concatenate([top, bottom], axis=0)


def remote(src, dst, send, recv, to):
    return pltpu.make_async_remote_copy(
        src_ref=src, dst_ref=dst, send_sem=send, recv_sem=recv, device_id=to, device_id_type=MESH)


def kernel(
    grads, owner, mom, update, renewed,
    who, raw, sib, r0, rz, momv, m1, m2s, m2r, m3s, m3r, gbuf, vbuf, gx, gr, gsend, grecv, rrecv, qbuf, idx_tab, val_tab,
    who_sem, raw_sem, mom_sem, sib_s, sib_r, t0_s, t0_r, z_s, z_r, m1_s, m1_r, m1_l, m2_ss, m2_rs, m3_ss, m3_rs,
    gx_s, gx_r, p_s, p_r, l_s, l_r, q_s, q_r,
):
    group = lax.axis_index("dp")
    f = lax.axis_index("fsdp")
    z, c = group // 2, group % 2
    me = (f // NA, f % NA)

    def z_of(step):
        return (z + step) % NZ

    def z_dev(d, core):
        return (z_of(1 if d == RIGHT else NZ - 1) * 2 + core, f)

    def plane(dy, dx):
        return ((me[0] + dy) % NA) * NA + (me[1] + dx) % NA

    def along(axis, step):
        return (group, plane(step, 0) if axis == 0 else plane(0, step))

    def on(axis, step):
        return (me[axis] + step) % NA

    def chunk(k):
        return pl.ds(pl.multiple_of(k * CHUNK, CHUNK), CHUNK)

    sibling = (z * 2 + 1 - c, f)

    who_copy = pltpu.make_async_copy(owner, who, who_sem)
    who_copy.start()
    raw_copy = [pltpu.make_async_copy(grads.at[z_of(j)], raw.at[z_of(j)], raw_sem.at[j]) for j in range(NZ)]
    for j in ORDER:
        raw_copy[j].start()
    mom_copy = pltpu.make_async_copy(mom, momv, mom_sem)
    mom_copy.start()

    barrier = pltpu.get_barrier_semaphore()
    peers = (sibling,) + tuple(z_dev(d, core) for d in (RIGHT, LEFT) for core in (c, 1 - c))
    peers += tuple((group, plane(dy, dx)) for dy, dx in OFFSETS)
    for peer in peers:
        pl.semaphore_signal(barrier, inc=1, device_id=peer, device_id_type=MESH)

    pl.semaphore_wait(barrier, len(peers))

    def t0_copies(k, q):
        return [
            remote(raw.at[z_of(4), core, :, chunk(k)], r0.at[k, i], t0_s.at[k, i], t0_r.at[k, i], z_dev(q, core))
            for i, core in enumerate((c, 1 - c))
        ]

    def z_copy(d, t, k):
        return remote(rz.at[d, t - 1, k], rz.at[d, t, k], z_s.at[d, t - 1, k], z_r.at[d, t - 1, k], z_dev(d, c))

    sib_copy = [
        None if j == 4 else remote(raw.at[z_of(j), 1 - c], sib.at[z_of(j)], sib_s.at[j], sib_r.at[j], sibling)
        for j in range(NZ)
    ]

    raw_copy[4].wait()
    for k in range(LEAD):
        for copy in t0_copies(k, k % 2):
            copy.start()
    for j in ORDER[1:]:
        raw_copy[j].wait()
        sib_copy[j].start()

    def m1_copy(h, j, first=0, count=MID):
        to = on(h, j)
        if h == 0:
            src = momv.at[:, to, :, pl.ds(first, count)]
        else:
            src = momv.at[:, :, to, pl.ds(MID + first, count)]
        dst = m1.at[h, me[h], :, :, pl.ds(first, count)]
        return remote(src, dst, m1_s.at[h, j - 1], m1_r.at[h, j - 1], along(h, j))

    def m1_local(h):
        if h == 0:
            src = momv.at[:, me[0], :, pl.ds(0, MID)]
        else:
            src = momv.at[:, :, me[1], pl.ds(MID, MID)]
        return pltpu.make_async_copy(src, m1.at[h, me[h]], m1_l.at[h])

    mom_copy.wait()
    for first in range(0, MID, SPLIT):
        for j in (2, 1, 3):
            for h in range(2):
                m1_copy(h, j, first, SPLIT).start()
    for h in range(2):
        m1_local(h).start()

    who_copy.wait()
    owners = [who[group * BLOCKS + m] for m in range(BLOCKS)]
    owner_at = ([lax.shift_right_logical(o, 2) for o in owners], [jnp.bitwise_and(o, 3) for o in owners])
    places = []
    for m in range(BLOCKS):
        place = jnp.int32(0)
        for earlier in range(m):
            place = place + jnp.where(owners[earlier] == owners[m], 1, 0).astype(jnp.int32)
        places.append(jnp.minimum(place, SLOTS - 1))
    keys = [owners[m] * SLOTS + places[m] for m in range(BLOCKS)]

    def table(slot, carry):
        index, valid = jnp.int32(0), jnp.float32(0)
        for m in range(BLOCKS):
            hit = keys[m] == slot
            index = jnp.where(hit, m, index)
            valid = jnp.where(hit, 1.0, valid)
        idx_tab[slot] = index
        val_tab[slot] = valid
        return carry

    lax.fori_loop(0, NF * SLOTS, table, 0)

    def held(h, step, m, first, count):
        b = 1 - h
        keep = jnp.where(owner_at[b][m] == me[b], 1.0, 0.0).astype(F32)
        return m1[h, owner_at[h][m], places[m], on(b, step), first:first + count, :] * keep

    def m2_copy(h, d):
        return remote(m2s.at[h, d], m2r.at[h, d], m2_ss.at[h, d], m2_rs.at[h, d], along(1 - h, 1 if d == RIGHT else 3))

    def m3_copy(h, d):
        return remote(m3s.at[h, d], m3r.at[h, d], m3_ss.at[h, d], m3_rs.at[h, d], along(1 - h, 1 if d == RIGHT else 3))

    QUARTER = MID // 2

    def merge_far():
        for h in range(2):
            for j in (1, 2, 3):
                m1_copy(h, j).wait_recv()
            m1_local(h).wait()
        for h in range(2):
            for d in (RIGHT, LEFT):
                for m in range(BLOCKS):
                    m2s[h, d, m] = held(h, 2, m, QUARTER * d, QUARTER)
                m2_copy(h, d).start()

    def merge_near():
        for h in range(2):
            for d in (RIGHT, LEFT):
                step = 1 if d == RIGHT else 3
                for m in range(BLOCKS):
                    m3s[h, d, m] = held(h, step, m, 0, MID)
                m2_copy(h, d).wait_recv()
                m3s[h, d, :, QUARTER * d:QUARTER * d + QUARTER, :] += m2r[h, d]
                m3_copy(h, d).start()

    def pair_sum(at, k):
        return raw[at, c, :, chunk(k), :].astype(F32) + sib[at, :, chunk(k), :].astype(F32)

    def hop(t, k, q):
        for d in (RIGHT, LEFT):
            step = 4 - t if d == RIGHT else NZ - 4 + t

            @pl.when(k == 0)
            def _():
                sib_copy[step].wait_recv()

            at = z_of(step)
            if t > 1:
                z_copy(d, t - 1, k).wait_recv()
                rz[d, t - 1, k] += pair_sum(at, k)
            elif d == q:
                for copy in t0_copies(k, q):
                    copy.wait_recv()
                rz[d, 0, k] = pair_sum(at, k) + (r0[k, 0].astype(F32) + r0[k, 1].astype(F32))
            else:
                rz[d, 0, k] = pair_sum(at, k)
            z_copy(d, t, k).start()

    def finish(k):
        z_copy(RIGHT, 3, k).wait_recv()
        z_copy(LEFT, 3, k).wait_recv()
        gbuf[:, chunk(k), :] = (pair_sum(z, k) + rz[RIGHT, 3, k] + rz[LEFT, 3, k]) * (1.0 / 16.0)

    def direct(first, count):
        rows = pl.ds(pl.multiple_of(first, CHUNK), count)

        def fill(to, carry):
            for s in range(SLOTS):
                gx[to, s, rows, :] = gbuf[idx_tab[to * SLOTS + s], rows, :] * val_tab[to * SLOTS + s]
            return carry

        lax.fori_loop(0, NF, fill, 0)
        for dy, dx in OFFSETS:
            to = plane(dy, dx)
            remote(gx.at[to, :, rows], gr.at[:, me[0], me[1], rows], gx_s, gx_r, (group, to)).start()
        gr[:, me[0], me[1], rows, :] = gx[f, :, rows, :]

    def velocity(first, count):
        for h in range(2):
            low, high = max(first, h * MID), min(first + count, (h + 1) * MID)
            if low >= high:
                continue
            at, n = low - h * MID, high - low
            for m in range(BLOCKS):
                state = held(h, 0, m, at, n) + m3r[h, RIGHT, m, at:at + n, :] + m3r[h, LEFT, m, at:at + n, :]
                vbuf[m, low:high, :] = (1.0 + RATE) * gbuf[m, low:high, :] + (RATE * RATE) * state

    def handler(b):
        return 2 * b + c

    def gram_copy(b):
        return remote(gsend.at[b], grecv.at[f], p_s.at[b], p_r, (group, handler(b)))

    def late_copy(i, b):
        rows = pl.ds(EARLY + i * CHUNK, CHUNK)
        return remote(vbuf.at[b, rows], rrecv.at[i, f], l_s.at[i, b], l_r.at[i], (group, handler(b)))

    def send_gram():
        for h in range(2):
            for d in (RIGHT, LEFT):
                m3_copy(h, d).wait_recv()
        velocity(0, EARLY)
        for b in range(BLOCKS):
            part = vbuf[b, 0:EARLY, :]
            body, diagonal = pack(dot_t(part, part))
            gsend[b, 0:R // 2, :] = body
            gsend[b, R // 2:PACKED, :] = diagonal

            @pl.when(handler(b) != f)
            def _():
                gram_copy(b).start()

    def send_late(i):
        velocity(EARLY + i * CHUNK, CHUNK)
        for b in range(BLOCKS):
            @pl.when(handler(b) != f)
            def _():
                late_copy(i, b).start()

    def when(k, run, low=0, high=NCH):
        @pl.when((k >= low) & (k < high))
        def _():
            run(k)

    last = NCH - 1

    def slots(sp, carry):
        for q in range(2):
            s = sp * 2 + q
            other = 1 - q
            when(s, lambda k: hop(1, k, q))
            when(s - 1, lambda k: hop(2, k, other))
            when(s - 2, lambda k: hop(3, k, q))

            @pl.when(s + LEAD < NCH)
            def _():
                for copy in t0_copies(s + LEAD, q):
                    copy.start()

            @pl.when(s == 3)
            def _():
                sib_copy[0].wait_recv()

            when(s - 3, finish)
            when(s - 3, lambda k: direct(k * CHUNK, CHUNK), 0, NCH - 2)
            for at, run in (
                (MERGE, merge_far), (NEAR, merge_near), (2 + EARLY_CH, send_gram),
            ) + tuple((3 + EARLY_CH + i, functools.partial(send_late, i)) for i in range(LATE_CH - 1)):
                if at % 2 == q:
                    @pl.when(s == at)
                    def _():
                        run()
        return carry

    lax.fori_loop(0, (NCH + 2) // 2, slots, 0)

    finish(last)
    send_late(LATE_CH - 1)
    direct((last - 1) * CHUNK, CHUNK)

    mine = f // 2
    handles = f % 2 == c

    def q_copy(to):
        return remote(qbuf.at[mine], qbuf.at[mine], q_s, q_r.at[mine], (group, to))

    @pl.when(handles)
    def _():
        grecv[f] = gsend[mine]
        for i in range(LATE_CH):
            rrecv[i, f] = vbuf[mine, EARLY + i * CHUNK:EARLY + (i + 1) * CHUNK, :]
        pltpu.make_async_copy(grecv.at[pl.ds(0, NF - 1)], grecv.at[pl.ds(0, NF - 1)], p_r).wait()
        total = grecv[0]
        for i in range(1, NF):
            total = total + grecv[i]
        gram = unpack(total[0:R // 2], total[R // 2:R // 2 + 1])
        for i in range(LATE_CH):
            pltpu.make_async_copy(rrecv.at[i, pl.ds(0, NF - 1)], rrecv.at[i, pl.ds(0, NF - 1)], l_r.at[i]).wait()
            late = rrecv[i].reshape(NF * CHUNK, R)
            gram = gram + dot_t(late, late)
        body, diagonal = pack(polynomial(gram))
        qbuf[mine, 0:R // 2, :] = body
        qbuf[mine, R // 2:PACKED, :] = diagonal
        for dy, dx in OFFSETS:
            q_copy(plane(dy, dx)).start()

    def receive_update():
        for b in range(BLOCKS):
            @pl.when(handler(b) != f)
            def _():
                pltpu.make_async_copy(qbuf.at[b], qbuf.at[b], q_r.at[b]).wait()

            update[b] = dot(vbuf[b], unpack(qbuf[b, 0:R // 2, :], qbuf[b, R // 2:R // 2 + 1, :]))

    def receive_gradient():
        part = gx.at[pl.ds(0, NF - 1)]
        pltpu.make_async_copy(part, part, gx_r).wait()
        for s in range(SLOTS):
            for a in range(NA):
                renewed[s, a] = RATE * momv[s, a] + gr[s, a]

    for b in range(BLOCKS):
        @pl.when(handler(b) != f)
        def _():
            gram_copy(b).wait_send()
            for i in range(LATE_CH):
                late_copy(i, b).wait_send()

    for j in ORDER[1:]:
        sib_copy[j].wait_send()
    for h in range(2):
        for j in (1, 2, 3):
            m1_copy(h, j).wait_send()
        for d in (RIGHT, LEFT):
            m2_copy(h, d).wait_send()
            m3_copy(h, d).wait_send()

    def drain(k, carry):
        for copy in t0_copies(k, 0):
            copy.wait_send()
        for d in (RIGHT, LEFT):
            for t in (1, 2, 3):
                z_copy(d, t, k).wait_send()
        return carry

    lax.fori_loop(0, NCH, drain, 0)
    direct(last * CHUNK, CHUNK)
    receive_update()
    receive_gradient()

    @pl.when(handles)
    def _():
        part = grecv.at[pl.ds(0, NF - 1)]
        pltpu.make_async_copy(part, part, q_s).wait()

    part = gx.at[pl.ds(0, NF - 1)]
    pltpu.make_async_copy(part, part, gx_s).wait()


def place(update, renewed, update_out, renewed_out, sem):
    copies = []
    for i in range(BLOCKS):
        copies.append(pltpu.make_async_copy(renewed.at[i // 4, i % 4], renewed_out.at[i // 4, i % 4], sem.at[i]))
    for i in range(2):
        half = pl.ds(i * (BLOCKS // 2), BLOCKS // 2)
        copies.append(pltpu.make_async_copy(update.at[half], update_out.at[half], sem.at[BLOCKS + i]))
    for copy in copies:
        copy.start()
    for copy in copies:
        copy.wait()


def local(grads, owner, momentum):
    raw = grads[0].reshape(NZ, 2, BLOCKS, PIECE, R)
    previous = momentum[0, 0].reshape(SLOTS, NA, NA, PIECE, R)
    dma = pltpu.SemaphoreType.DMA

    def hbm(array):
        return pltpu.with_memory_space_constraint(array, pltpu.HBM)

    update, renewed = pl.pallas_call(
        kernel,
        out_shape=(
            pltpu.VMEM((BLOCKS, PIECE, R), F32),
            pltpu.VMEM((SLOTS, NA, NA, PIECE, R), F32),
        ),
        in_specs=[
            pl.BlockSpec(memory_space=pl.ANY),
            pl.BlockSpec(memory_space=pl.ANY),
            pl.BlockSpec(memory_space=pl.ANY),
        ],
        out_specs=(pl.BlockSpec(memory_space=pltpu.VMEM), pl.BlockSpec(memory_space=pltpu.VMEM)),
        scratch_shapes=[
            pltpu.SMEM((NF * BLOCKS,), jnp.int32),
            pltpu.VMEM((NZ, 2, BLOCKS, PIECE, R), jnp.bfloat16),
            pltpu.VMEM((NZ, BLOCKS, PIECE, R), jnp.bfloat16),
            pltpu.VMEM((NCH, 2, BLOCKS, CHUNK, R), jnp.bfloat16),
            pltpu.VMEM((2, 4, NCH, BLOCKS, CHUNK, R), F32),
            pltpu.VMEM((SLOTS, NA, NA, PIECE, R), F32),
            pltpu.VMEM((2, NA, SLOTS, NA, MID, R), F32),
            pltpu.VMEM((2, 2, BLOCKS, MID // 2, R), F32),
            pltpu.VMEM((2, 2, BLOCKS, MID // 2, R), F32),
            pltpu.VMEM((2, 2, BLOCKS, MID, R), F32),
            pltpu.VMEM((2, 2, BLOCKS, MID, R), F32),
            pltpu.VMEM((BLOCKS, PIECE, R), F32),
            pltpu.VMEM((BLOCKS, PIECE, R), F32),
            pltpu.VMEM((NF, SLOTS, PIECE, R), F32),
            pltpu.VMEM((SLOTS, NA, NA, PIECE, R), F32),
            pltpu.VMEM((BLOCKS, PACKED, R), F32),
            pltpu.VMEM((NF, PACKED, R), F32),
            pltpu.VMEM((LATE_CH, NF, CHUNK, R), F32),
            pltpu.VMEM((BLOCKS, PACKED, R), F32),
            pltpu.SMEM((NF * SLOTS,), jnp.int32),
            pltpu.SMEM((NF * SLOTS,), F32),
            dma, dma((NZ,)), dma, dma((NZ,)), dma((NZ,)),
            dma((NCH, 2)), dma((NCH, 2)), dma((2, 3, NCH)), dma((2, 3, NCH)),
            dma((2, 3)), dma((2, 3)), dma((2,)), dma((2, 2)), dma((2, 2)), dma((2, 2)), dma((2, 2)),
            dma, dma,
            dma((BLOCKS,)), dma, dma((LATE_CH, BLOCKS)), dma((LATE_CH,)), dma, dma((BLOCKS,)),
        ],
        compiler_params=pltpu.CompilerParams(
            collective_id=0, has_side_effects=True, vmem_limit_bytes=48 * 2**20),
    )(hbm(raw), hbm(owner[:, 0]), hbm(previous))
    update, renewed = pl.pallas_call(
        place,
        out_shape=(
            jax.ShapeDtypeStruct((BLOCKS, PIECE, R), F32),
            jax.ShapeDtypeStruct((SLOTS, NA, NA, PIECE, R), F32),
        ),
        in_specs=[pl.BlockSpec(memory_space=pl.ANY)] * 2,
        out_specs=(pl.BlockSpec(memory_space=pl.ANY),) * 2,
        scratch_shapes=[dma((BLOCKS + 2,))],
    )(pltpu.with_memory_space_constraint(update, pltpu.VMEM), pltpu.with_memory_space_constraint(renewed, pltpu.VMEM))
    return update, renewed.reshape(1, 1, SLOTS, D, R)


def solution(mesh):
    return jax.shard_map(
        local,
        mesh=mesh,
        in_specs=(P("dp", None, "fsdp", None), P(), P("dp", "fsdp", None, None, None)),
        out_specs=(P("dp", "fsdp", None), P("dp", "fsdp", None, None, None)),
        check_vma=False,
    )
```

```python
import functools
import math

import jax
import jax.numpy as jnp
from jax import lax
from jax.experimental import pallas as pl
from jax.experimental.pallas import tpu as pltpu
from jax.sharding import PartitionSpec as P

MESH = pl.DeviceIdType.MESH
F32 = jnp.float32

NZ = 8
NA = 4
NF = NA * NA
BLOCKS = 8
SLOTS = 2
D = 2560
R = 128
PIECE = D // NF
CHUNK = 16
HALF = CHUNK // 2
NCH = PIECE // CHUNK
MID = PIECE // 2
EARLY_CH = 6
EARLY = EARLY_CH * CHUNK
LATE_CH = NCH - EARLY_CH
LEAD = 4
MERGE = 3
NEAR = 5
SPLIT = 80
PACKED = 72
ITERS = 3

COEF_A = 3.4445
COEF_B = -4.775
COEF_C = 2.0315
RATE = 0.95

OFFSETS = ((2, 2), (0, 2), (2, 0), (1, 2), (2, 1), (3, 2), (2, 3), (1, 1), (3, 3), (1, 3), (3, 1), (0, 1), (1, 0), (0, 3), (3, 0))
ORDER = (4, 3, 5, 2, 6, 1, 7, 0)
RIGHT, LEFT = 0, 1


def dot(a, b):
    return lax.dot_general(a, b, (((1,), (0,)), ((), ())), precision=lax.Precision.HIGHEST, preferred_element_type=F32)


def dot_t(a, b):
    return lax.dot_general(a, b, (((0,), (0,)), ((), ())), precision=lax.Precision.HIGHEST, preferred_element_type=F32)


def polynomial(gram):
    rows = lax.broadcasted_iota(jnp.int32, (R, R), 0)
    cols = lax.broadcasted_iota(jnp.int32, (R, R), 1)
    eye = jnp.where(rows == cols, 1.0, 0.0).astype(F32)
    total = jnp.sum(jnp.sum(gram * eye, axis=1, keepdims=True), axis=0, keepdims=True)
    inv = 1.0 / (jnp.sqrt(total) + 1e-07)
    gram = (gram * inv) * inv
    product = None
    for sweep in range(ITERS):
        poly = COEF_A * eye + COEF_B * gram + COEF_C * dot(gram, gram)
        product = poly if product is None else dot(product, poly)
        if sweep < ITERS - 1:
            gram = dot(poly, dot(gram, poly))
    return (0.2 * math.sqrt(D)) * inv * product


def pack(matrix):
    rows = lax.broadcasted_iota(jnp.int32, (R // 2, R), 0)
    cols = lax.broadcasted_iota(jnp.int32, (R // 2, R), 1)
    top, bottom = matrix[:R // 2], matrix[R // 2:]
    body = jnp.where(rows > cols, pltpu.roll(bottom, R // 2, 1), top)
    diagonal = jnp.sum(jnp.where(rows == cols - R // 2, bottom, 0.0), axis=0, keepdims=True)
    return body, jnp.broadcast_to(diagonal, (PACKED - R // 2, R))


def unpack(body, diagonal):
    rows = lax.broadcasted_iota(jnp.int32, (R // 2, R), 0)
    cols = lax.broadcasted_iota(jnp.int32, (R // 2, R), 1)
    turned = jnp.concatenate([body, jnp.zeros_like(body)], axis=0).T
    left = turned[:R // 2]
    top = jnp.where(rows <= cols, body, left)
    last = jnp.where(rows > cols - R // 2, pltpu.roll(body, R // 2, 1), pltpu.roll(left, R // 2, 1))
    last = jnp.where(rows == cols - R // 2, diagonal, last)
    bottom = jnp.where(cols < R // 2, turned[R // 2:], last)
    return jnp.concatenate([top, bottom], axis=0)


def remote(src, dst, send, recv, to):
    return pltpu.make_async_remote_copy(
        src_ref=src, dst_ref=dst, send_sem=send, recv_sem=recv, device_id=to, device_id_type=MESH)


def kernel(
    grads, owner, mom, update, renewed,
    who, raw, sib, r0, rz, momv, m1, m2s, m2r, m3s, m3r, gbuf, vbuf, gx, gr, gsend, grecv, rrecv, held_gram, qbuf, idx_tab, val_tab,
    who_sem, raw_sem, mom_sem, sib_s, sib_r, t0_s, t0_r, z_s, z_r, m1_s, m1_r, m1_l, m2_ss, m2_rs, m3_ss, m3_rs,
    gx_s, gx_r, p_s, p_r, l_s, l_r, q_s, q_r,
):
    group = lax.axis_index("dp")
    f = lax.axis_index("fsdp")
    z, c = group // 2, group % 2
    me = (f // NA, f % NA)

    def z_of(step):
        return (z + step) % NZ

    def z_dev(d, core):
        return (z_of(1 if d == RIGHT else NZ - 1) * 2 + core, f)

    def plane(dy, dx):
        return ((me[0] + dy) % NA) * NA + (me[1] + dx) % NA

    def along(axis, step):
        return (group, plane(step, 0) if axis == 0 else plane(0, step))

    def on(axis, step):
        return (me[axis] + step) % NA

    def chunk(k):
        return pl.ds(pl.multiple_of(k * CHUNK, CHUNK), CHUNK)

    sibling = (z * 2 + 1 - c, f)

    who_copy = pltpu.make_async_copy(owner, who, who_sem)
    who_copy.start()
    raw_copy = [pltpu.make_async_copy(grads.at[z_of(j)], raw.at[z_of(j)], raw_sem.at[j]) for j in range(NZ)]
    for j in ORDER:
        raw_copy[j].start()
    mom_copy = pltpu.make_async_copy(mom, momv, mom_sem)
    mom_copy.start()

    barrier = pltpu.get_barrier_semaphore()
    peers = (sibling,) + tuple(z_dev(d, core) for d in (RIGHT, LEFT) for core in (c, 1 - c))
    peers += tuple((group, plane(dy, dx)) for dy, dx in OFFSETS)
    for peer in peers:
        pl.semaphore_signal(barrier, inc=1, device_id=peer, device_id_type=MESH)

    pl.semaphore_wait(barrier, len(peers))

    def t0_copies(k, q):
        return [
            remote(raw.at[z_of(4), core, :, chunk(k)], r0.at[k, i], t0_s.at[k, i], t0_r.at[k, i], z_dev(q, core))
            for i, core in enumerate((c, 1 - c))
        ]

    def z_copy(d, t, k):
        return remote(rz.at[d, t - 1, k], rz.at[d, t, k], z_s.at[d, t - 1, k], z_r.at[d, t - 1, k], z_dev(d, c))

    sib_copy = [
        None if j == 4 else remote(raw.at[z_of(j), 1 - c], sib.at[z_of(j)], sib_s.at[j], sib_r.at[j], sibling)
        for j in range(NZ)
    ]

    raw_copy[4].wait()
    for k in range(LEAD):
        for copy in t0_copies(k, k % 2):
            copy.start()
    for j in ORDER[1:]:
        raw_copy[j].wait()
        sib_copy[j].start()

    def m1_copy(h, j, first=0, count=MID):
        to = on(h, j)
        if h == 0:
            src = momv.at[:, to, :, pl.ds(first, count)]
        else:
            src = momv.at[:, :, to, pl.ds(MID + first, count)]
        dst = m1.at[h, me[h], :, :, pl.ds(first, count)]
        return remote(src, dst, m1_s.at[h, j - 1], m1_r.at[h, j - 1], along(h, j))

    def m1_local(h):
        if h == 0:
            src = momv.at[:, me[0], :, pl.ds(0, MID)]
        else:
            src = momv.at[:, :, me[1], pl.ds(MID, MID)]
        return pltpu.make_async_copy(src, m1.at[h, me[h]], m1_l.at[h])

    mom_copy.wait()
    for first in range(0, MID, SPLIT):
        for j in (2, 1, 3):
            for h in range(2):
                m1_copy(h, j, first, SPLIT).start()
    for h in range(2):
        m1_local(h).start()

    who_copy.wait()
    owners = [who[group * BLOCKS + m] for m in range(BLOCKS)]
    owner_at = ([lax.shift_right_logical(o, 2) for o in owners], [jnp.bitwise_and(o, 3) for o in owners])
    places = []
    for m in range(BLOCKS):
        place = jnp.int32(0)
        for earlier in range(m):
            place = place + jnp.where(owners[earlier] == owners[m], 1, 0).astype(jnp.int32)
        places.append(jnp.minimum(place, SLOTS - 1))
    keys = [owners[m] * SLOTS + places[m] for m in range(BLOCKS)]

    def table(slot, carry):
        index, valid = jnp.int32(0), jnp.float32(0)
        for m in range(BLOCKS):
            hit = keys[m] == slot
            index = jnp.where(hit, m, index)
            valid = jnp.where(hit, 1.0, valid)
        idx_tab[slot] = index
        val_tab[slot] = valid
        return carry

    lax.fori_loop(0, NF * SLOTS, table, 0)

    def held(h, step, m, first, count):
        b = 1 - h
        keep = jnp.where(owner_at[b][m] == me[b], 1.0, 0.0).astype(F32)
        return m1[h, owner_at[h][m], places[m], on(b, step), first:first + count, :] * keep

    def m2_copy(h, d):
        return remote(m2s.at[h, d], m2r.at[h, d], m2_ss.at[h, d], m2_rs.at[h, d], along(1 - h, 1 if d == RIGHT else 3))

    def m3_copy(h, d):
        return remote(m3s.at[h, d], m3r.at[h, d], m3_ss.at[h, d], m3_rs.at[h, d], along(1 - h, 1 if d == RIGHT else 3))

    QUARTER = MID // 2

    def merge_far():
        for h in range(2):
            for j in (1, 2, 3):
                m1_copy(h, j).wait_recv()
            m1_local(h).wait()
        for h in range(2):
            for d in (RIGHT, LEFT):
                for m in range(BLOCKS):
                    m2s[h, d, m] = held(h, 2, m, QUARTER * d, QUARTER)
                m2_copy(h, d).start()

    def merge_near():
        for h in range(2):
            for d in (RIGHT, LEFT):
                step = 1 if d == RIGHT else 3
                for m in range(BLOCKS):
                    m3s[h, d, m] = held(h, step, m, 0, MID)
                m2_copy(h, d).wait_recv()
                m3s[h, d, :, QUARTER * d:QUARTER * d + QUARTER, :] += m2r[h, d]
                m3_copy(h, d).start()

    def pair_sum(at, k):
        return raw[at, c, :, chunk(k), :].astype(F32) + sib[at, :, chunk(k), :].astype(F32)

    def hop(t, k, q):
        for d in (RIGHT, LEFT):
            step = 4 - t if d == RIGHT else NZ - 4 + t

            @pl.when(k == 0)
            def _():
                sib_copy[step].wait_recv()

            at = z_of(step)
            if t > 1:
                z_copy(d, t - 1, k).wait_recv()
                rz[d, t - 1, k] += pair_sum(at, k)
            elif d == q:
                for copy in t0_copies(k, q):
                    copy.wait_recv()
                rz[d, 0, k] = pair_sum(at, k) + (r0[k, 0].astype(F32) + r0[k, 1].astype(F32))
            else:
                rz[d, 0, k] = pair_sum(at, k)
            z_copy(d, t, k).start()

    def finish(k):
        z_copy(RIGHT, 3, k).wait_recv()
        z_copy(LEFT, 3, k).wait_recv()
        gbuf[:, chunk(k), :] = (pair_sum(z, k) + rz[RIGHT, 3, k] + rz[LEFT, 3, k]) * (1.0 / 16.0)

    def direct(first, count):
        rows = pl.ds(pl.multiple_of(first, CHUNK), count)

        def fill(to, carry):
            for s in range(SLOTS):
                gx[to, s, rows, :] = gbuf[idx_tab[to * SLOTS + s], rows, :] * val_tab[to * SLOTS + s]
            return carry

        lax.fori_loop(0, NF, fill, 0)
        for dy, dx in OFFSETS:
            to = plane(dy, dx)
            remote(gx.at[to, :, rows], gr.at[:, me[0], me[1], rows], gx_s, gx_r, (group, to)).start()
        gr[:, me[0], me[1], rows, :] = gx[f, :, rows, :]

    def velocity(first, count):
        for h in range(2):
            low, high = max(first, h * MID), min(first + count, (h + 1) * MID)
            if low >= high:
                continue
            at, n = low - h * MID, high - low
            for m in range(BLOCKS):
                state = held(h, 0, m, at, n) + m3r[h, RIGHT, m, at:at + n, :] + m3r[h, LEFT, m, at:at + n, :]
                vbuf[m, low:high, :] = (1.0 + RATE) * gbuf[m, low:high, :] + (RATE * RATE) * state

    def handler(b):
        return 2 * b + c

    def gram_copy(b):
        return remote(gsend.at[b], grecv.at[f], p_s.at[b], p_r, (group, handler(b)))

    def late_copy(i, b):
        rows = pl.ds(EARLY + i * CHUNK, CHUNK)
        return remote(vbuf.at[b, rows], rrecv.at[i, f], l_s.at[i, b], l_r.at[i], (group, handler(b)))

    def send_gram():
        for h in range(2):
            for d in (RIGHT, LEFT):
                m3_copy(h, d).wait_recv()
        velocity(0, EARLY)
        for b in range(BLOCKS):
            part = vbuf[b, 0:EARLY, :]
            body, diagonal = pack(dot_t(part, part))
            gsend[b, 0:R // 2, :] = body
            gsend[b, R // 2:PACKED, :] = diagonal

            @pl.when(handler(b) != f)
            def _():
                gram_copy(b).start()

    def send_late(i):
        velocity(EARLY + i * CHUNK, CHUNK)
        for b in range(BLOCKS):
            @pl.when(handler(b) != f)
            def _():
                late_copy(i, b).start()

    def when(k, run, low=0, high=NCH):
        @pl.when((k >= low) & (k < high))
        def _():
            run(k)

    last = NCH - 1

    def slots(sp, carry):
        for q in range(2):
            s = sp * 2 + q
            other = 1 - q
            when(s, lambda k: hop(1, k, q))
            when(s - 1, lambda k: hop(2, k, other))
            when(s - 2, lambda k: hop(3, k, q))

            @pl.when(s + LEAD < NCH)
            def _():
                for copy in t0_copies(s + LEAD, q):
                    copy.start()

            @pl.when(s == 3)
            def _():
                sib_copy[0].wait_recv()

            when(s - 3, finish)
            when(s - 3, lambda k: direct(k * CHUNK, CHUNK), 0, NCH - 2)
            for at, run in (
                (MERGE, merge_far), (NEAR, merge_near), (2 + EARLY_CH, send_gram),
            ) + tuple((3 + EARLY_CH + i, functools.partial(send_late, i)) for i in range(LATE_CH - 1)):
                if at % 2 == q:
                    @pl.when(s == at)
                    def _():
                        run()
        return carry

    lax.fori_loop(0, (NCH + 2) // 2, slots, 0)

    mine = f // 2
    handles = f % 2 == c

    def late_gram(i):
        rrecv[i, f] = vbuf[mine, EARLY + i * CHUNK:EARLY + (i + 1) * CHUNK, :]
        pltpu.make_async_copy(rrecv.at[i, pl.ds(0, NF - 1)], rrecv.at[i, pl.ds(0, NF - 1)], l_r.at[i]).wait()
        late = rrecv[i].reshape(NF * CHUNK, R)
        return dot_t(late, late)

    @pl.when(handles)
    def _():
        grecv[f] = gsend[mine]
        pltpu.make_async_copy(grecv.at[pl.ds(0, NF - 1)], grecv.at[pl.ds(0, NF - 1)], p_r).wait()
        total = grecv[0]
        for i in range(1, NF):
            total = total + grecv[i]
        gram = unpack(total[0:R // 2], total[R // 2:R // 2 + 1])
        for i in range(LATE_CH - 2):
            gram = gram + late_gram(i)
        held_gram[...] = gram

    finish(last)
    send_late(LATE_CH - 1)
    direct((last - 1) * CHUNK, CHUNK)

    def q_copy(to):
        return remote(qbuf.at[mine], qbuf.at[mine], q_s, q_r.at[mine], (group, to))

    @pl.when(handles)
    def _():
        gram = held_gram[...]
        for i in range(LATE_CH - 2, LATE_CH):
            gram = gram + late_gram(i)
        body, diagonal = pack(polynomial(gram))
        qbuf[mine, 0:R // 2, :] = body
        qbuf[mine, R // 2:PACKED, :] = diagonal
        for dy, dx in OFFSETS:
            q_copy(plane(dy, dx)).start()

    def receive_update():
        for b in range(BLOCKS):
            @pl.when(handler(b) != f)
            def _():
                pltpu.make_async_copy(qbuf.at[b], qbuf.at[b], q_r.at[b]).wait()

            update[b] = dot(vbuf[b], unpack(qbuf[b, 0:R // 2, :], qbuf[b, R // 2:R // 2 + 1, :]))

    def receive_gradient():
        part = gx.at[pl.ds(0, NF - 1)]
        pltpu.make_async_copy(part, part, gx_r).wait()
        for s in range(SLOTS):
            for a in range(NA):
                renewed[s, a] = RATE * momv[s, a] + gr[s, a]

    for b in range(BLOCKS):
        @pl.when(handler(b) != f)
        def _():
            gram_copy(b).wait_send()
            for i in range(LATE_CH):
                late_copy(i, b).wait_send()

    for j in ORDER[1:]:
        sib_copy[j].wait_send()
    for h in range(2):
        for j in (1, 2, 3):
            m1_copy(h, j).wait_send()
        for d in (RIGHT, LEFT):
            m2_copy(h, d).wait_send()
            m3_copy(h, d).wait_send()

    def drain(k, carry):
        for copy in t0_copies(k, 0):
            copy.wait_send()
        for d in (RIGHT, LEFT):
            for t in (1, 2, 3):
                z_copy(d, t, k).wait_send()
        return carry

    lax.fori_loop(0, NCH, drain, 0)
    direct(last * CHUNK, CHUNK)
    receive_update()
    receive_gradient()

    @pl.when(handles)
    def _():
        part = grecv.at[pl.ds(0, NF - 1)]
        pltpu.make_async_copy(part, part, q_s).wait()

    part = gx.at[pl.ds(0, NF - 1)]
    pltpu.make_async_copy(part, part, gx_s).wait()


def place(update, renewed, update_out, renewed_out, sem):
    copies = []
    for i in range(BLOCKS):
        copies.append(pltpu.make_async_copy(renewed.at[i // 4, i % 4], renewed_out.at[i // 4, i % 4], sem.at[i]))
    for i in range(2):
        half = pl.ds(i * (BLOCKS // 2), BLOCKS // 2)
        copies.append(pltpu.make_async_copy(update.at[half], update_out.at[half], sem.at[BLOCKS + i]))
    for copy in copies:
        copy.start()
    for copy in copies:
        copy.wait()


def local(grads, owner, momentum):
    raw = grads[0].reshape(NZ, 2, BLOCKS, PIECE, R)
    previous = momentum[0, 0].reshape(SLOTS, NA, NA, PIECE, R)
    dma = pltpu.SemaphoreType.DMA

    def hbm(array):
        return pltpu.with_memory_space_constraint(array, pltpu.HBM)

    update, renewed = pl.pallas_call(
        kernel,
        out_shape=(
            pltpu.VMEM((BLOCKS, PIECE, R), F32),
            pltpu.VMEM((SLOTS, NA, NA, PIECE, R), F32),
        ),
        in_specs=[
            pl.BlockSpec(memory_space=pl.ANY),
            pl.BlockSpec(memory_space=pl.ANY),
            pl.BlockSpec(memory_space=pl.ANY),
        ],
        out_specs=(pl.BlockSpec(memory_space=pltpu.VMEM), pl.BlockSpec(memory_space=pltpu.VMEM)),
        scratch_shapes=[
            pltpu.SMEM((NF * BLOCKS,), jnp.int32),
            pltpu.VMEM((NZ, 2, BLOCKS, PIECE, R), jnp.bfloat16),
            pltpu.VMEM((NZ, BLOCKS, PIECE, R), jnp.bfloat16),
            pltpu.VMEM((NCH, 2, BLOCKS, CHUNK, R), jnp.bfloat16),
            pltpu.VMEM((2, 4, NCH, BLOCKS, CHUNK, R), F32),
            pltpu.VMEM((SLOTS, NA, NA, PIECE, R), F32),
            pltpu.VMEM((2, NA, SLOTS, NA, MID, R), F32),
            pltpu.VMEM((2, 2, BLOCKS, MID // 2, R), F32),
            pltpu.VMEM((2, 2, BLOCKS, MID // 2, R), F32),
            pltpu.VMEM((2, 2, BLOCKS, MID, R), F32),
            pltpu.VMEM((2, 2, BLOCKS, MID, R), F32),
            pltpu.VMEM((BLOCKS, PIECE, R), F32),
            pltpu.VMEM((BLOCKS, PIECE, R), F32),
            pltpu.VMEM((NF, SLOTS, PIECE, R), F32),
            pltpu.VMEM((SLOTS, NA, NA, PIECE, R), F32),
            pltpu.VMEM((BLOCKS, PACKED, R), F32),
            pltpu.VMEM((NF, PACKED, R), F32),
            pltpu.VMEM((LATE_CH, NF, CHUNK, R), F32),
            pltpu.VMEM((R, R), F32),
            pltpu.VMEM((BLOCKS, PACKED, R), F32),
            pltpu.SMEM((NF * SLOTS,), jnp.int32),
            pltpu.SMEM((NF * SLOTS,), F32),
            dma, dma((NZ,)), dma, dma((NZ,)), dma((NZ,)),
            dma((NCH, 2)), dma((NCH, 2)), dma((2, 3, NCH)), dma((2, 3, NCH)),
            dma((2, 3)), dma((2, 3)), dma((2,)), dma((2, 2)), dma((2, 2)), dma((2, 2)), dma((2, 2)),
            dma, dma,
            dma((BLOCKS,)), dma, dma((LATE_CH, BLOCKS)), dma((LATE_CH,)), dma, dma((BLOCKS,)),
        ],
        compiler_params=pltpu.CompilerParams(
            collective_id=0, has_side_effects=True, vmem_limit_bytes=48 * 2**20),
    )(hbm(raw), hbm(owner[:, 0]), hbm(previous))
    update, renewed = pl.pallas_call(
        place,
        out_shape=(
            jax.ShapeDtypeStruct((BLOCKS, PIECE, R), F32),
            jax.ShapeDtypeStruct((SLOTS, NA, NA, PIECE, R), F32),
        ),
        in_specs=[pl.BlockSpec(memory_space=pl.ANY)] * 2,
        out_specs=(pl.BlockSpec(memory_space=pl.ANY),) * 2,
        scratch_shapes=[dma((BLOCKS + 2,))],
    )(pltpu.with_memory_space_constraint(update, pltpu.VMEM), pltpu.with_memory_space_constraint(renewed, pltpu.VMEM))
    return update, renewed.reshape(1, 1, SLOTS, D, R)


def solution(mesh):
    return jax.shard_map(
        local,
        mesh=mesh,
        in_specs=(P("dp", None, "fsdp", None), P(), P("dp", "fsdp", None, None, None)),
        out_specs=(P("dp", "fsdp", None), P("dp", "fsdp", None, None, None)),
        check_vma=False,
    )
```
